128 devices in a mesh: seq: 16 (over y, x_lo, core), fsdp: 8 (over x_hi, z).
Axes of the slice: x: 4 (x_hi: 2, x_lo: 2; x = x_hi * 2 + x_lo), y: 4, z: 4, core: 2. Of those that a mesh axis runs over, the one named last changes fastest.
Arguments:
- q_nope: bfloat16 [2048, 16384], P('seq', 'fsdp'), may hold values from -6 to 6
- q_rope: bfloat16 [2048, 8192], P('seq', 'fsdp'), may hold values from -8 to 8
- latent_t: bfloat16 [512, 2048], P(None, 'seq'), may hold values from -6 to 6
- k_rope_t: bfloat16 [64, 2048], P(None, 'seq'), may hold values from -8 to 8
- w_uk: bfloat16 [512, 16384], P('seq', 'fsdp'), may hold values from -0.25 to 0.25
- w_uv: bfloat16 [512, 16384], P('seq', 'fsdp'), may hold values from -0.25 to 0.25
- grad_out: bfloat16 [2048, 16384], P('seq', 'fsdp'), may hold values from -6 to 6
- seg_ids: int32 [2048], replicated, may hold values from 0 to 7, as said below
- anc_flags: int32 [16, 16], replicated, may hold values from 0 to 1, as said below
Outputs:
- attn_out: bfloat16 [2048, 16384], P('seq', 'fsdp')
- d_q_nope: bfloat16 [2048, 16384], P('seq', 'fsdp')
- d_q_rope: bfloat16 [2048, 8192], P('seq', 'fsdp')
- d_latent_t: bfloat16 [512, 2048], P(None, 'seq')
- d_k_rope_t: bfloat16 [64, 2048], P(None, 'seq')
- d_w_uk: float32 [512, 16384], P('seq', 'fsdp')
- d_w_uv: float32 [512, 16384], P('seq', 'fsdp')
The draws below stay inside these ranges and needn't reach their ends.
Inputs may be any that keep to these rules, and one draw needn't show every extreme that they name: seg_ids start at 0, never fall, are constant over each aligned run of 128 tokens and rise by at most one from one run to the next; segment 0 is an ancestor of every other segment. anc_flags[a, b] is 1 exactly where the segment of block b is a strict ancestor of the segment of block a in a tree of segments whose parents come earlier, so only where b < a.
All inputs are finite; a program needn't handle non-finite values.
Results may differ from the reference program's by a relative error of at most 0.035.
Values may be sent and summed in bfloat16 or wider, within the bound.
A program may use at most 128 MiB of HBM per device.

```python
import math
import jax
import jax.numpy as jnp
from jax import lax

HEADS = 128
LATENT = 512
ROPE = 64
NOPE = 128
VDIM = 128
BLOCK = 128
TOKENS = 2048
NBLK = 16


def block_tree(key):
    start_key, parent_key = jax.random.split(key)
    ranking = jax.random.permutation(start_key, NBLK - 1).astype(jnp.int32)
    rest = (ranking < NBLK // 2 - 1).astype(jnp.int32)
    starts = jnp.concatenate([jnp.ones((1,), jnp.int32), rest])
    seg_block = jnp.cumsum(starts).astype(jnp.int32) - 1
    order = jnp.arange(NBLK, dtype=jnp.int32)
    parent = jax.random.randint(parent_key, (NBLK,), 0, jnp.maximum(order, 1), dtype=jnp.int32)
    reach = ((order[None, :] == parent[:, None]) & (order[:, None] > 0)).astype(jnp.int32)
    for repeat_num in range(NBLK.bit_length() + 1):
        reach = (reach + jnp.dot(reach, reach) > 0).astype(jnp.int32)
    flags = reach[seg_block][:, seg_block]
    return (seg_block, flags)


def draw_seg_ids(key, part):
    seg_block, flags = block_tree(key)
    return jnp.repeat(seg_block, BLOCK).astype(jnp.int32)


def draw_anc_flags(key, part):
    seg_block, flags = block_tree(key)
    return flags.astype(jnp.int32)


def draw_q_rope(key, part):
    key = jax.random.fold_in(key, 31)
    values = jnp.clip(jax.random.normal(key, (TOKENS, HEADS, ROPE), jnp.float32), -4.0, 4.0)
    return values.reshape(TOKENS, HEADS * ROPE).astype(jnp.bfloat16)


def draw_k_rope_t(key, part):
    key = jax.random.fold_in(key, 37)
    values = jnp.clip(jax.random.normal(key, (TOKENS, ROPE), jnp.float32), -4.0, 4.0)
    return values.T.astype(jnp.bfloat16)


def shard_levels(stream_key, dims, pieces, smallest, largest):
    gain, own = 1.0, jax.random.fold_in(stream_key, 6)
    for axis_at, blocks in pieces:
        heights = jnp.exp(jax.random.uniform(jax.random.fold_in(own, axis_at), (blocks,), jnp.float32, smallest / len(pieces), largest / len(pieces)))
        gain = gain * jnp.repeat(heights, dims[axis_at] // blocks).reshape([-1 if axis == axis_at else 1 for axis in range(len(dims))])
    return gain


def scatter_about(key, shape, deviation, limit, cuts=(), kind=jnp.bfloat16):
    factor_of = shard_levels(key, shape, cuts, -0.22, 0.18) if cuts else 1.0
    array = jax.random.normal(key, shape, jnp.float32) * deviation * factor_of
    return jnp.minimum(jnp.maximum(array, -limit), limit).astype(kind)


def setup_inputs(seed: int = 0) -> dict:
    arg_keys = jax.random.split(jax.random.key(seed), 10)
    return {
        "q_nope": scatter_about(arg_keys[0], (TOKENS, HEADS * NOPE), 1.0, 6.0, ((0, 16), (1, 8))),
        "q_rope": draw_q_rope(jax.random.fold_in(arg_keys[9], 71), 0),
        "latent_t": scatter_about(arg_keys[2], (LATENT, TOKENS), 1.0, 6.0, ((1, 16),)),
        "k_rope_t": draw_k_rope_t(jax.random.fold_in(arg_keys[9], 71), 0),
        "w_uk": scatter_about(arg_keys[4], (LATENT, HEADS * NOPE), LATENT ** -0.5, 0.25, ((0, 16), (1, 8))),
        "w_uv": scatter_about(arg_keys[5], (LATENT, HEADS * VDIM), LATENT ** -0.5, 0.25, ((0, 16), (1, 8))),
        "grad_out": scatter_about(arg_keys[6], (TOKENS, HEADS * VDIM), 1.0, 6.0, ((0, 16), (1, 8))),
        "seg_ids": draw_seg_ids(jax.random.fold_in(arg_keys[9], 71), 0),
        "anc_flags": draw_anc_flags(jax.random.fold_in(arg_keys[9], 71), 0),
    }


def reference(q_nope, q_rope, latent_t, k_rope_t, w_uk, w_uv, grad_out, seg_ids, anc_flags):
    score_scale = 1.0 / math.sqrt(NOPE + ROPE)
    positions = jnp.arange(TOKENS, dtype=jnp.int32)
    block_of = positions // BLOCK
    flag_tok = anc_flags[block_of][:, block_of]
    visible = (seg_ids[:, None] == seg_ids[None, :]) & (positions[None, :] <= positions[:, None]) | (flag_tok == 1)
    nope_heads = q_nope.reshape(TOKENS, HEADS, NOPE).transpose(1, 0, 2)
    rope_heads = q_rope.reshape(TOKENS, HEADS, ROPE).transpose(1, 0, 2)
    grad_heads = grad_out.reshape(TOKENS, HEADS, VDIM).transpose(1, 0, 2)
    uk_heads = w_uk.reshape(LATENT, HEADS, NOPE).transpose(1, 0, 2)
    uv_heads = w_uv.reshape(LATENT, HEADS, VDIM).transpose(1, 0, 2)

    def per_head(state_now, inputs):
        lat_acc, rope_acc = state_now
        nope_one, rope_one, grad_one, uk_one, uv_one = inputs
        q_abs = jnp.dot(nope_one, uk_one.T, preferred_element_type=jnp.float32).astype(jnp.bfloat16)
        scores = (jnp.dot(q_abs, latent_t, preferred_element_type=jnp.float32) + jnp.dot(rope_one, k_rope_t, preferred_element_type=jnp.float32)) * score_scale
        masked = jnp.where(visible, scores, -jnp.inf)
        row_max = lax.optimization_barrier(jnp.max(masked, axis=1, keepdims=True))
        exponent = jnp.where(visible, jnp.exp(masked - row_max), 0.0)
        probabilities = exponent / lax.optimization_barrier(jnp.sum(exponent, axis=1, keepdims=True))
        rounded = probabilities.astype(jnp.bfloat16)
        o_lat = jnp.dot(rounded, latent_t.T, preferred_element_type=jnp.float32).astype(jnp.bfloat16)
        out_one = jnp.dot(o_lat, uv_one, preferred_element_type=jnp.float32).astype(jnp.bfloat16)
        grad_uv = jnp.dot(o_lat.T, grad_one, preferred_element_type=jnp.float32)
        d_o_lat = jnp.dot(grad_one, uv_one.T, preferred_element_type=jnp.float32).astype(jnp.bfloat16)
        row_delta = lax.optimization_barrier(jnp.sum(d_o_lat.astype(jnp.float32) * o_lat.astype(jnp.float32), axis=1, keepdims=True))
        grad_prob = jnp.dot(d_o_lat, latent_t, preferred_element_type=jnp.float32)
        grad_score = (probabilities * (grad_prob - row_delta) * score_scale).astype(jnp.bfloat16)
        grad_abs = jnp.dot(grad_score, latent_t.T, preferred_element_type=jnp.float32).astype(jnp.bfloat16)
        grad_rope = jnp.dot(grad_score, k_rope_t.T, preferred_element_type=jnp.float32).astype(jnp.bfloat16)
        lat_acc = lat_acc + jnp.dot(q_abs.T, grad_score, preferred_element_type=jnp.float32) + jnp.dot(d_o_lat.T, rounded, preferred_element_type=jnp.float32)
        rope_acc = rope_acc + jnp.dot(rope_one.T, grad_score, preferred_element_type=jnp.float32)
        grad_nope = jnp.dot(grad_abs, uk_one, preferred_element_type=jnp.float32).astype(jnp.bfloat16)
        grad_uk = jnp.dot(grad_abs.T, nope_one, preferred_element_type=jnp.float32)
        return ((lat_acc, rope_acc), (out_one, grad_nope, grad_rope, grad_uk, grad_uv))
    start_state = (jnp.zeros((LATENT, TOKENS), jnp.float32), jnp.zeros((ROPE, TOKENS), jnp.float32))
    finals, stacked = lax.scan(per_head, start_state, (nope_heads, rope_heads, grad_heads, uk_heads, uv_heads))
    out_all, nope_all, rope_all, uk_all, uv_all = stacked
    attn_out = out_all.transpose(1, 0, 2).reshape(TOKENS, HEADS * VDIM)
    d_q_nope = nope_all.transpose(1, 0, 2).reshape(TOKENS, HEADS * NOPE)
    d_q_rope = rope_all.transpose(1, 0, 2).reshape(TOKENS, HEADS * ROPE)
    d_w_uk = uk_all.transpose(1, 0, 2).reshape(LATENT, HEADS * NOPE)
    d_w_uv = uv_all.transpose(1, 0, 2).reshape(LATENT, HEADS * VDIM)
    d_latent_t = finals[0].astype(jnp.bfloat16)
    d_k_rope_t = finals[1].astype(jnp.bfloat16)
    return (attn_out, d_q_nope, d_q_rope, d_latent_t, d_k_rope_t, d_w_uk, d_w_uv)
```

```python
import functools
import math

import jax
import jax.numpy as jnp
from jax import lax
from jax.experimental import pallas as pl
from jax.experimental.pallas import tpu as pltpu
from jax.sharding import PartitionSpec as P

F32, BF16 = jnp.float32, jnp.bfloat16
MESH = pl.DeviceIdType.MESH
NEG = -1e30
SCALE = 1.0 / math.sqrt(192.0)
SCALE_LOG2E = SCALE * math.log2(math.e)
TILES = 8
PART = 144

SEQ_PEERS = [
    (dy, dx, dc) for dy in (1, 3, 0, 2) for dx in (0, 1) for dc in (0, 1) if (dy, dx, dc) != (0, 0, 0)
]
CHIP_PEERS = [(0, 1), (1, 0), (3, 0), (1, 1), (3, 1), (2, 0), (2, 1)]


def dot(left, right):
    return lax.dot_general(left, right, (((1,), (0,)), ((), ())), preferred_element_type=F32)


def unpack_rope(x):
    return jnp.concatenate([x[:, :64], x[:, 64:]], axis=0)


def pack_rope(x):
    return jnp.concatenate([x[:64], x[64:]], axis=1)


def tile_of(lat, t, lo, hi):
    return jnp.concatenate([lat[0, t, lo:hi, :], lat[1, t, lo:hi, :]], axis=1)


def fused(
    seg, anc, qn_in, qr_in, lt_in, kr_in, uk_in, uv_in, g_in,
    ro, rw, fin,
    lat, sw, iw, sq, iq, wt, wtT, kcT, vT, kc, v, sc, dk, dv, so, dl, ra, sa, rb, sb, rc, dws,
    l1s, l1r, l2s, l2r, l3s, l3r, iws, iwr, iqs, iqr, os, orr, ras, rar, rbs, rbr, rcs, rcr, ws, wr, es, er,
):
    s, f = lax.axis_index("seq"), lax.axis_index("fsdp")
    y, x, c = s // 4, (s // 2) % 2, s % 2
    k = s // 2
    h, z = f // 4, f % 4

    def seq_peer(rel):
        return ((y + rel[0]) % 4) * 4 + ((x + rel[1]) % 2) * 2 + (c + rel[2]) % 2

    def chip_peer(rel):
        return ((y + rel[0]) % 4) * 2 + (x + rel[1]) % 2

    def z_peer(dz):
        return (z + dz) % 4

    other_core = (k * 2 + 1 - c, f)
    zrow = pl.multiple_of(z * PART, 16)

    def remote(src, dst, ssem, rsem, device):
        return pltpu.make_async_remote_copy(
            src_ref=src, dst_ref=dst, send_sem=ssem, recv_sem=rsem, device_id=device, device_id_type=MESH
        )

    bar = pltpu.get_barrier_semaphore()
    peers = [(seq_peer(r), f) for r in SEQ_PEERS]
    peers += [(s, h * 4 + z_peer(dz)) for dz in (1, 2, 3)]
    peers += [(chip_peer(r) * 2 + c, (1 - h) * 4 + z) for r in [(0, 0)] + CHIP_PEERS]
    for p in peers:
        pl.semaphore_signal(bar, inc=1, device_id=p, device_id_type=MESH)

    lat[c, k, 0:512, :] = lt_in[...]
    lat[c, k, 512:576, :] = kr_in[...]
    for d in range(16):
        sw[d, 0:32, :] = uk_in[:, 128 * d : 128 * d + 128]
        sw[d, 32:64, :] = uv_in[:, 128 * d : 128 * d + 128]
        sq[d, 0:128, :] = qn_in[:, 128 * d : 128 * d + 128]
        sq[d, 128:256, :] = g_in[:, 128 * d : 128 * d + 128]
    for pair in range(8):
        both = qr_in[:, 128 * pair : 128 * pair + 128].astype(F32)
        sq[2 * pair, 256:320, :] = pack_rope(both[:, :64]).astype(BF16)
        sq[2 * pair + 1, 256:320, :] = pack_rope(both[:, 64:]).astype(BF16)
    iw[s] = sw[s]
    iq[s] = sq[s]
    pl.semaphore_wait(bar, len(peers))

    sends = []

    for i, r in enumerate(CHIP_PEERS):
        cp = remote(
            lat.at[c, k, pl.ds(zrow, PART)], lat.at[c, k, pl.ds(zrow, PART)],
            l1s.at[i], l1r.at[k], (chip_peer(r) * 2 + c, f),
        )
        cp.start()
        sends.append(cp)
    cp = remote(lat.at[c, k], lat.at[c, k], l3s.at[k], l3r.at[k], other_core)
    cp.start()
    sends.append(cp)
    for i, r in enumerate(SEQ_PEERS):
        p = seq_peer(r)
        cp = remote(sw.at[p], iw.at[s], iws.at[i], iwr.at[s], (p, f))
        cp.start()
        sends.append(cp)
    for i, r in enumerate(SEQ_PEERS):
        p = seq_peer(r)
        cp = remote(sq.at[p], iq.at[s], iqs.at[i], iqr.at[s], (p, f))
        cp.start()
        sends.append(cp)
    for i, r in enumerate(CHIP_PEERS):
        q = chip_peer(r)
        piece = lat.at[c, q, pl.ds(zrow, PART)]
        remote(piece, piece, l1s.at[i], l1r.at[q], other_core).wait_recv()
        for j, dz in enumerate((1, 3, 2)):
            cp = remote(piece, piece, l2s.at[3 * i + j], l2r.at[4 * q + z], (s, h * 4 + z_peer(dz)))
            cp.start()
            sends.append(cp)
    for i, r in enumerate(CHIP_PEERS):
        q = chip_peer(r)
        for dz in (1, 3, 2):
            zz = z_peer(dz)
            piece = lat.at[c, q, pl.ds(pl.multiple_of(zz * PART, 16), PART)]
            remote(piece, piece, l2s.at[0], l2r.at[4 * q + zz], other_core).wait_recv()
        cp = remote(lat.at[c, q], lat.at[c, q], l3s.at[q], l3r.at[q], other_core)
        cp.start()
        sends.append(cp)

    for r in SEQ_PEERS:
        p = seq_peer(r)
        remote(iw.at[p], iw.at[p], iws.at[0], iwr.at[p], other_core).wait_recv()
    for d in range(16):
        wt[0, 32 * d : 32 * d + 32, :] = iw[d, 0:32, :]
        wt[1, 32 * d : 32 * d + 32, :] = iw[d, 32:64, :]
    wtT[0:128, :] = wt[0].astype(F32).T.astype(BF16)
    wtT[128:256, :] = wt[1].astype(F32).T.astype(BF16)
    for r in [(0, 0)] + CHIP_PEERS:
        q = chip_peer(r)
        block = lat.at[1 - c, q]
        remote(block, block, l3s.at[0], l3r.at[q], other_core).wait_recv()

    for t in range(TILES):
        rope = tile_of(lat, t, 512, 576)
        kv = dot(wtT[...], tile_of(lat, t, 0, 512))
        kcT[t, 0:128, :] = kv[:128].astype(BF16)
        kcT[t, 128:192, :] = rope
        vT[t] = kv[128:].astype(BF16)
        kc[t, :, 0:128] = kv[:128].T.astype(BF16)
        kc[t, :, 128:192] = rope.astype(F32).T.astype(BF16)
        v[t] = kv[128:].T.astype(BF16)

    lane = lax.broadcasted_iota(jnp.int32, (1, 256), 1)

    def bias_of(a, b):
        seen = (seg[128 * a] == seg[128 * b]) | (anc[a, b] == 1)
        return jnp.where(seen, 0.0, NEG).astype(F32)

    def attend(I):
        a0, a1 = iq[2 * I], iq[2 * I + 1]
        qn = jnp.concatenate([a0[0:128], a1[0:128]], axis=0)
        g = jnp.concatenate([a0[128:256], a1[128:256]], axis=0)
        qr = jnp.concatenate(
            [unpack_rope(a0[256:320].astype(F32)), unpack_rope(a1[256:320].astype(F32))], axis=0
        )
        qT = jnp.concatenate([qn.astype(F32).T, qr.T], axis=0).astype(BF16)
        qc = jnp.concatenate([qn, qr.astype(BF16)], axis=1)
        gT32 = g.astype(F32).T
        gT = gT32.astype(BF16)
        top = jnp.full((1, 256), NEG, F32)
        for J in range(I + 1):
            scores = dot(kc[J], qT)
            if J < I:
                halves = []
                for b in range(2):
                    bias = jnp.where(
                        lane < 128, bias_of(2 * I, 2 * J + b), bias_of(2 * I + 1, 2 * J + b)
                    )
                    halves.append(scores[128 * b : 128 * b + 128] + bias)
                scores = jnp.concatenate(halves, axis=0)
            else:
                key = lax.broadcasted_iota(jnp.int32, (256, 256), 0)
                query = lax.broadcasted_iota(jnp.int32, (256, 256), 1)
                bias = jnp.where(lane < 128, 0.0, bias_of(2 * I + 1, 2 * I))
                scores = jnp.concatenate([scores[:128] + bias, scores[128:]], axis=0)
                scores = jnp.where(key <= query, scores, NEG)
            sc[J] = scores
            top = jnp.maximum(top, jnp.max(scores, axis=0, keepdims=True))
        top = top * SCALE_LOG2E
        total = jnp.zeros((1, 256), F32)
        oT = jnp.zeros((128, 256), F32)
        for J in range(I + 1):
            weight = jnp.exp2(sc[J] * SCALE_LOG2E - top)
            total = total + jnp.sum(weight, axis=0, keepdims=True)
            sc[J] = weight
            oT = oT + dot(vT[J], weight.astype(BF16))
        inverse = 1.0 / total
        oT = oT * inverse
        delta = jnp.sum(oT * gT32, axis=0, keepdims=True)
        dqT = jnp.zeros((192, 256), F32)
        for J in range(I + 1):
            prob = sc[J] * inverse
            ds = (prob * (dot(v[J], gT) - delta)).astype(BF16)
            dqT = dqT + dot(kcT[J], ds)
            dk_now = dot(ds, qc)
            dv_now = dot(prob.astype(BF16), g)
            if I == TILES - 1:
                dk[J] = dk_now
                dv[J] = dv_now
            else:
                dk[J] += dk_now
                dv[J] += dv_now
        o = oT.T.astype(BF16)
        dqT = dqT * SCALE
        dqn = dqT[:128].T.astype(BF16)
        dqr = dqT[128:].T
        for e in range(2):
            lo = 128 * e
            so[2 * I + e, 0:128, :] = o[lo : lo + 128]
            so[2 * I + e, 128:256, :] = dqn[lo : lo + 128]
            so[2 * I + e, 256:320, :] = pack_rope(dqr[lo : lo + 128]).astype(BF16)

    def send_out(I):
        for e in range(2):
            d = 2 * I + e

            @pl.when(s != d)
            def _():
                remote(so.at[d], ro.at[s], os.at[d], orr.at[s], (d, f)).start()

            @pl.when(s == d)
            def _():
                ro[s] = so[d]

    def key_grads(I, w_grad):
        dkt = dk[I] * SCALE
        kv = jnp.concatenate([dkt[:, :128], dv[I]], axis=1)
        w = jnp.concatenate([wt[0], wt[1]], axis=1)
        lat_grad = dot(w, kv.T.astype(BF16)).astype(BF16)
        rope_grad = dkt[:, 128:].T.astype(BF16)
        for e in range(2):
            dl[e, I, 0:512, :] = lat_grad[:, 128 * e : 128 * e + 128]
            dl[e, I, 512:576, :] = rope_grad[:, 128 * e : 128 * e + 128]
        remote(dl.at[1 - c, I], ra.at[I], ras.at[I], rar.at[I], other_core).start()
        return w_grad + dot(tile_of(lat, I, 0, 512), kv.astype(BF16))

    def stage_b(I):
        remote(ra.at[I], ra.at[I], ras.at[I], rar.at[I], other_core).wait_recv()
        sa[I] = (dl[c, I].astype(F32) + ra[I].astype(F32)).astype(BF16)
        for j, dz in enumerate((1, 3, 2)):
            zz = z_peer(dz)
            remote(
                sa.at[I, pl.ds(pl.multiple_of(zz * PART, 16), PART)], rb.at[I, z],
                rbs.at[3 * I + j], rbr.at[4 * I + z], (s, h * 4 + zz),
            ).start()

    def stage_c(I):
        acc = sa[I, pl.ds(zrow, PART), :].astype(F32)
        for dz in (1, 3, 2):
            zz = z_peer(dz)
            remote(rb.at[I, zz], rb.at[I, zz], rbs.at[3 * I], rbr.at[4 * I + zz], other_core).wait_recv()
            acc = acc + rb[I, zz].astype(F32)
        sb[I] = acc.astype(BF16)
        dest = 2 * I + c
        slot = h * 8 + k

        @pl.when(k != I)
        def _():
            remote(sb.at[I], rc.at[slot], rcs.at[2 * I], rcr.at[slot], (dest, f)).start()

        @pl.when(k == I)
        def _():
            rc[slot] = sb[I]

        remote(sb.at[I], rc.at[slot], rcs.at[2 * I + 1], rcr.at[slot], (dest, (1 - h) * 4 + z)).start()

    w_grad = jnp.zeros((512, 256), F32)
    for I in reversed(range(TILES)):
        for e in range(2):
            d = 2 * I + e

            @pl.when(s != d)
            def _():
                remote(iq.at[d], iq.at[d], iqs.at[0], iqr.at[d], other_core).wait_recv()

        attend(I)
        w_grad = key_grads(I, w_grad)
        send_out(I)
        if I + 1 < TILES:
            stage_b(I + 1)
        if I + 2 < TILES:
            stage_c(I + 2)
    stage_c(1)
    stage_b(0)
    w_grad = w_grad.astype(BF16)
    for d in range(16):
        dws[d, 0:32, :] = w_grad[32 * d : 32 * d + 32, :128]
        dws[d, 32:64, :] = w_grad[32 * d : 32 * d + 32, 128:]
    for i, r in enumerate(SEQ_PEERS):
        p = seq_peer(r)
        cp = remote(dws.at[p], rw.at[s], ws.at[i], wr.at[s], (p, f))
        cp.start()
        sends.append(cp)
    rw[s] = dws[s]
    stage_c(0)

    acc = rc[h * 8 + k].astype(F32)
    for hh in (h, 1 - h):
        for r in [(0, 0)] + CHIP_PEERS:
            slot = hh * 8 + chip_peer(r)
            if hh is h and r == (0, 0):
                continue
            remote(rc.at[slot], rc.at[slot], rcs.at[0], rcr.at[slot], other_core).wait_recv()
            acc = acc + rc[slot].astype(F32)
    fin[pl.ds(zrow, PART), :] = acc.astype(BF16)
    for j, dz in enumerate((1, 3, 2)):
        piece = fin.at[pl.ds(zrow, PART)]
        cp = remote(piece, piece, es.at[j], er.at[z], (s, h * 4 + z_peer(dz)))
        cp.start()
        sends.append(cp)

    for r in SEQ_PEERS:
        p = seq_peer(r)
        remote(ro.at[p], ro.at[p], os.at[0], orr.at[p], other_core).wait_recv()
        remote(rw.at[p], rw.at[p], ws.at[0], wr.at[p], other_core).wait_recv()
    for dz in (1, 3, 2):
        zz = z_peer(dz)
        piece = fin.at[pl.ds(pl.multiple_of(zz * PART, 16), PART)]
        remote(piece, piece, es.at[0], er.at[zz], other_core).wait_recv()
    for cp in sends:
        cp.wait_send()
    for I in range(TILES):
        remote(ra.at[I], ra.at[I], ras.at[I], rar.at[I], other_core).wait_send()
        for j in range(3):
            remote(rb.at[I, 0], rb.at[I, 0], rbs.at[3 * I + j], rbr.at[0], other_core).wait_send()

        @pl.when(k != I)
        def _():
            remote(sb.at[I], sb.at[I], rcs.at[2 * I], rcr.at[0], other_core).wait_send()

        remote(sb.at[I], sb.at[I], rcs.at[2 * I + 1], rcr.at[0], other_core).wait_send()
        for e in range(2):
            d = 2 * I + e

            @pl.when(s != d)
            def _():
                remote(so.at[d], so.at[d], os.at[d], orr.at[0], other_core).wait_send()


def unpack(ro, rw, fin, out, dqn, dqr, dlat, dkr, duk, duv):
    for d in range(16):
        cols = slice(128 * d, 128 * d + 128)
        out[:, cols] = ro[d, 0:128, :]
        dqn[:, cols] = ro[d, 128:256, :]
        duk[:, cols] = rw[d, 0:32, :].astype(F32)
        duv[:, cols] = rw[d, 32:64, :].astype(F32)
    for pair in range(8):
        both = [unpack_rope(ro[2 * pair + e, 256:320, :].astype(F32)) for e in range(2)]
        dqr[:, 128 * pair : 128 * pair + 128] = jnp.concatenate(both, axis=1).astype(BF16)
    dlat[...] = fin[0:512, :]
    dkr[...] = fin[512:576, :]


def on_device(q_nope, q_rope, latent_t, k_rope_t, w_uk, w_uv, grad_out, seg_ids, anc_flags):
    vmem = pl.BlockSpec(memory_space=pltpu.VMEM)
    smem = pl.BlockSpec(memory_space=pltpu.SMEM)
    dma = pltpu.SemaphoreType.DMA
    sem_counts = [7, 8, 21, 32, 8, 8, 15, 16, 15, 16, 16, 16, 8, 8, 24, 32, 16, 16, 15, 16, 3, 4]
    parts = pl.pallas_call(
        fused,
        out_shape=[
            jax.ShapeDtypeStruct((16, 320, 128), BF16),
            jax.ShapeDtypeStruct((16, 64, 128), BF16),
            jax.ShapeDtypeStruct((576, 128), BF16),
        ],
        in_specs=[smem, smem] + [vmem] * 7,
        out_specs=[vmem] * 3,
        scratch_shapes=[
            pltpu.VMEM((2, 8, 576, 128), BF16),
            pltpu.VMEM((16, 64, 128), BF16),
            pltpu.VMEM((16, 64, 128), BF16),
            pltpu.VMEM((16, 320, 128), BF16),
            pltpu.VMEM((16, 320, 128), BF16),
            pltpu.VMEM((2, 512, 128), BF16),
            pltpu.VMEM((256, 512), BF16),
            pltpu.VMEM((8, 192, 256), BF16),
            pltpu.VMEM((8, 128, 256), BF16),
            pltpu.VMEM((8, 256, 192), BF16),
            pltpu.VMEM((8, 256, 128), BF16),
            pltpu.VMEM((8, 256, 256), F32),
            pltpu.VMEM((8, 256, 192), F32),
            pltpu.VMEM((8, 256, 128), F32),
            pltpu.VMEM((16, 320, 128), BF16),
            pltpu.VMEM((2, 8, 576, 128), BF16),
            pltpu.VMEM((8, 576, 128), BF16),
            pltpu.VMEM((8, 576, 128), BF16),
            pltpu.VMEM((8, 4, PART, 128), BF16),
            pltpu.VMEM((8, PART, 128), BF16),
            pltpu.VMEM((16, PART, 128), BF16),
            pltpu.VMEM((16, 64, 128), BF16),
        ]
        + [dma((n,)) for n in sem_counts],
        compiler_params=pltpu.CompilerParams(
            collective_id=0, has_side_effects=True, vmem_limit_bytes=56 * 1024 * 1024
        ),
        name="attention_exchange",
    )(seg_ids, anc_flags, q_nope, q_rope, latent_t, k_rope_t, w_uk, w_uv, grad_out)
    bf, fl = BF16, F32
    return pl.pallas_call(
        unpack,
        out_shape=[
            jax.ShapeDtypeStruct((128, 2048), bf),
            jax.ShapeDtypeStruct((128, 2048), bf),
            jax.ShapeDtypeStruct((128, 1024), bf),
            jax.ShapeDtypeStruct((512, 128), bf),
            jax.ShapeDtypeStruct((64, 128), bf),
            jax.ShapeDtypeStruct((32, 2048), fl),
            jax.ShapeDtypeStruct((32, 2048), fl),
        ],
        in_specs=[vmem] * 3,
        out_specs=[vmem] * 7,
        compiler_params=pltpu.CompilerParams(vmem_limit_bytes=32 * 1024 * 1024),
        name="unpack",
    )(*parts)


def solution(mesh):
    placed = (
        P("seq", "fsdp"),
        P("seq", "fsdp"),
        P(None, "seq"),
        P(None, "seq"),
        P("seq", "fsdp"),
        P("seq", "fsdp"),
        P("seq", "fsdp"),
        P(),
        P(),
    )
    return jax.shard_map(
        on_device,
        mesh=mesh,
        in_specs=placed,
        out_specs=(
            P("seq", "fsdp"),
            P("seq", "fsdp"),
            P("seq", "fsdp"),
            P(None, "seq"),
            P(None, "seq"),
            P("seq", "fsdp"),
            P("seq", "fsdp"),
        ),
        check_vma=False,
    )
```

```python
import functools
import math

import jax
import jax.numpy as jnp
from jax import lax
from jax.experimental import pallas as pl
from jax.experimental.pallas import tpu as pltpu
from jax.sharding import PartitionSpec as P

F32, BF16 = jnp.float32, jnp.bfloat16
MESH = pl.DeviceIdType.MESH
NEG = -1e30
SCALE = 1.0 / math.sqrt(192.0)
SCALE_LOG2E = SCALE * math.log2(math.e)
TILES = 8
LAG = 2
PART = 144
ALONG_Z = 448
PART_Z = ALONG_Z // 4
REST = 576 - ALONG_Z
PART_REST = REST // 4

SEQ_PEERS = [
    (dy, dx, dc) for dy in (0, 3, 1, 2) for dx in (0, 1) for dc in (0, 1) if (dy, dx, dc) != (0, 0, 0)
]
CHIP_PEERS = [(0, 1), (1, 0), (3, 0), (1, 1), (3, 1), (2, 0), (2, 1)]


def dot(left, right):
    return lax.dot_general(left, right, (((1,), (0,)), ((), ())), preferred_element_type=F32)


def unpack_rope(x):
    return jnp.concatenate([x[:, :64], x[:, 64:]], axis=0)


def pack_rope(x):
    return jnp.concatenate([x[:64], x[64:]], axis=1)


def tile_of(lat, t, lo, hi):
    return jnp.concatenate([lat[0, t, lo:hi, :], lat[1, t, lo:hi, :]], axis=1)


def fused(
    seg, anc, qn_hbm, qr_hbm, lt_hbm, kr_hbm, uk_hbm, uv_hbm, g_hbm,
    ro, rw, fe,
    qn_in, qr_in, uk_in, uv_in, g_in,
    lat, sw, iw, sq, iq, wt, wtT, kcT, vT, kc, v, sc, dss, ps, qcs, gcs, dks, dvs, kvs, so, sdw, dl, ra, sa,
    rb, sb, rc, ry, sy, rz, part, other, whole,
    ins, own, l1s, l1r, l2s, l2r, l3s, l3r, iws, iwr, iqs, iqr, os, orr, ras, rar, rbs, rbr, rcs, rcr,
    rys, ryr, rzs, rzr, hs, hr, ws, wr, es, er,
):
    s, f = lax.axis_index("seq"), lax.axis_index("fsdp")
    y, x, c = s // 4, (s // 2) % 2, s % 2
    k = s // 2
    h, z = f // 4, f % 4

    def seq_peer(rel):
        return ((y + rel[0]) % 4) * 4 + ((x + rel[1]) % 2) * 2 + (c + rel[2]) % 2

    def chip_peer(rel):
        return ((y + rel[0]) % 4) * 2 + (x + rel[1]) % 2

    def z_peer(dz):
        return (z + dz) % 4

    other_core = (k * 2 + 1 - c, f)
    zrow = pl.multiple_of(z * PART, 16)

    def remote(src, dst, ssem, rsem, device):
        return pltpu.make_async_remote_copy(
            src_ref=src, dst_ref=dst, send_sem=ssem, recv_sem=rsem, device_id=device, device_id_type=MESH
        )

    loads = [
        pltpu.make_async_copy(src, dst, ins.at[i])
        for i, (src, dst) in enumerate(
            [
                (lt_hbm, lat.at[c, k, pl.ds(0, 512)]),
                (kr_hbm, lat.at[c, k, pl.ds(512, 64)]),
                (uk_hbm, uk_in),
                (uv_hbm, uv_in),
                (qn_hbm, qn_in),
                (qr_hbm, qr_in),
                (g_hbm, g_in),
            ]
        )
    ]
    for cp in loads:
        cp.start()

    bar = pltpu.get_barrier_semaphore()
    peers = [(seq_peer(r), f) for r in SEQ_PEERS]
    peers += [(s, h * 4 + z_peer(dz)) for dz in (1, 2, 3)]
    peers += [(s, (1 - h) * 4 + z)]
    for p in peers:
        pl.semaphore_signal(bar, inc=1, device_id=p, device_id_type=MESH)

    for cp in loads:
        cp.wait()
    for d in range(16):
        sw[d, 0:32, :] = uk_in[:, 128 * d : 128 * d + 128]
        sw[d, 32:64, :] = uv_in[:, 128 * d : 128 * d + 128]
        sq[d, 0:128, :] = qn_in[:, 128 * d : 128 * d + 128]
        sq[d, 192:320, :] = g_in[:, 128 * d : 128 * d + 128]
    for pair in range(8):
        both = qr_in[:, 128 * pair : 128 * pair + 128].astype(F32)
        sq[2 * pair, 128:192, :] = pack_rope(both[:, :64]).astype(BF16)
        sq[2 * pair + 1, 128:192, :] = pack_rope(both[:, 64:]).astype(BF16)
    iw[s] = sw[s]
    iq[s] = sq[s]
    pl.semaphore_wait(bar, len(peers))

    sends = []

    for i, r in enumerate(CHIP_PEERS):
        cp = remote(
            lat.at[c, k, pl.ds(zrow, PART)], lat.at[c, k, pl.ds(zrow, PART)],
            l1s.at[i], l1r.at[k], (chip_peer(r) * 2 + c, f),
        )
        cp.start()
        sends.append(cp)
    cp = remote(lat.at[c, k], lat.at[c, k], l3s.at[k], l3r.at[k], other_core)
    cp.start()
    sends.append(cp)
    for i, r in enumerate(CHIP_PEERS):
        q = chip_peer(r)
        piece = lat.at[c, q, pl.ds(zrow, PART)]
        remote(piece, piece, l1s.at[i], l1r.at[q], other_core).wait_recv()
        for j, dz in enumerate((1, 3, 2)):
            cp = remote(piece, piece, l2s.at[3 * i + j], l2r.at[4 * q + z], (s, h * 4 + z_peer(dz)))
            cp.start()
            sends.append(cp)
    for i, r in enumerate(SEQ_PEERS):
        p = seq_peer(r)
        cp = remote(sw.at[p], iw.at[s], iws.at[i], iwr.at[s], (p, f))
        cp.start()
        sends.append(cp)
    for i, r in enumerate(SEQ_PEERS):
        p = seq_peer(r)
        cp = remote(sq.at[p], iq.at[s], iqs.at[i], iqr.at[s], (p, f))
        cp.start()
        sends.append(cp)
    for r in SEQ_PEERS:
        p = seq_peer(r)
        remote(iw.at[p], iw.at[p], iws.at[0], iwr.at[p], other_core).wait_recv()
    for d in range(16):
        wt[0, 32 * d : 32 * d + 32, :] = iw[d, 0:32, :]
        wt[1, 32 * d : 32 * d + 32, :] = iw[d, 32:64, :]
    wtT[0:128, :] = wt[0].astype(F32).T.astype(BF16)
    wtT[128:256, :] = wt[1].astype(F32).T.astype(BF16)

    for i, r in enumerate(CHIP_PEERS):
        q = chip_peer(r)
        for dz in (1, 3, 2):
            zz = z_peer(dz)
            piece = lat.at[c, q, pl.ds(pl.multiple_of(zz * PART, 16), PART)]
            remote(piece, piece, l2s.at[0], l2r.at[4 * q + zz], other_core).wait_recv()
        cp = remote(lat.at[c, q], lat.at[c, q], l3s.at[q], l3r.at[q], other_core)
        cp.start()
        sends.append(cp)


    for r in [(0, 0)] + CHIP_PEERS:
        t = chip_peer(r)
        block = lat.at[1 - c, t]
        remote(block, block, l3s.at[0], l3r.at[t], other_core).wait_recv()
        rope = tile_of(lat, t, 512, 576)
        kv = dot(wtT[...], tile_of(lat, t, 0, 512))
        kcT[t, 0:128, :] = kv[:128].astype(BF16)
        kcT[t, 128:192, :] = rope
        vT[t] = kv[128:].astype(BF16)
        kc[t, :, 0:128] = kv[:128].T.astype(BF16)
        kc[t, :, 128:192] = rope.astype(F32).T.astype(BF16)
        v[t] = kv[128:].T.astype(BF16)

    lane = lax.broadcasted_iota(jnp.int32, (1, 256), 1)

    def bias_of(a, b):
        seen = (seg[128 * a] == seg[128 * b]) | (anc[a, b] == 1)
        return jnp.where(seen, 0.0, NEG).astype(F32)

    def pair_index(I, J):
        return I * (I + 1) // 2 + J

    def query_tile(I):
        a0, a1 = iq[2 * I], iq[2 * I + 1]
        qn = jnp.concatenate([a0[0:128], a1[0:128]], axis=0)
        g = jnp.concatenate([a0[192:320], a1[192:320]], axis=0)
        qr = jnp.concatenate(
            [unpack_rope(a0[128:192].astype(F32)), unpack_rope(a1[128:192].astype(F32))], axis=0
        )
        qT = jnp.concatenate([qn.astype(F32).T, qr.T], axis=0).astype(BF16)
        qcs[I] = jnp.concatenate([qn, qr.astype(BF16)], axis=1)
        gcs[I] = g
        gT = g.astype(F32).T
        top = jnp.full((1, 256), NEG, F32)
        for J in range(I + 1):
            scores = dot(kc[J], qT)
            if J < I:
                halves = []
                for b in range(2):
                    bias = jnp.where(
                        lane < 128, bias_of(2 * I, 2 * J + b), bias_of(2 * I + 1, 2 * J + b)
                    )
                    halves.append(scores[128 * b : 128 * b + 128] + bias)
                scores = jnp.concatenate(halves, axis=0)
            else:
                key = lax.broadcasted_iota(jnp.int32, (256, 256), 0)
                query = lax.broadcasted_iota(jnp.int32, (256, 256), 1)
                bias = jnp.where(lane < 128, 0.0, bias_of(2 * I + 1, 2 * I))
                scores = jnp.concatenate([scores[:128] + bias, scores[128:]], axis=0)
                scores = jnp.where(key <= query, scores, NEG)
            sc[J] = scores
            top = jnp.maximum(top, jnp.max(scores, axis=0, keepdims=True))
        top = top * SCALE_LOG2E
        total = jnp.zeros((1, 256), F32)
        oT = jnp.zeros((128, 256), F32)
        for J in range(I + 1):
            weight = jnp.exp2(sc[J] * SCALE_LOG2E - top)
            total = total + jnp.sum(weight, axis=0, keepdims=True)
            sc[J] = weight
            oT = oT + dot(vT[J], weight.astype(BF16))
        inverse = 1.0 / total
        oT = oT * inverse
        delta = jnp.sum(oT * gT, axis=0, keepdims=True)
        gT = gT.astype(BF16)
        dqT = jnp.zeros((192, 256), F32)
        for J in range(I + 1):
            prob = sc[J] * inverse
            ds = (prob * (dot(v[J], gT) - delta)).astype(BF16)
            dss[pair_index(I, J)] = ds
            ps[pair_index(I, J)] = prob.astype(BF16)
            dqT = dqT + dot(kcT[J], ds)
        dqT = dqT * SCALE
        o = oT.T.astype(BF16)
        dqn = dqT[:128].T.astype(BF16)
        dqr = dqT[128:].T
        for e in range(2):
            lo = 128 * e
            so[2 * I + e, 0:128, :] = o[lo : lo + 128]
            so[2 * I + e, 128:256, :] = dqn[lo : lo + 128]
            so[2 * I + e, 256:320, :] = pack_rope(dqr[lo : lo + 128]).astype(BF16)

    def backward_keys(J):
        dk = jnp.zeros((256, 192), F32)
        dv = jnp.zeros((256, 128), F32)
        for I in range(J, TILES):
            dk = dk + dot(dss[pair_index(I, J)], qcs[I])
            dv = dv + dot(ps[pair_index(I, J)], gcs[I])
        dk = dk * SCALE
        dks[...] = dk
        dvs[...] = dv

    def key_grads(J):
        dk = dks[...]
        kv = jnp.concatenate([dk[:, :128], dvs[...]], axis=1)
        kvs[J] = kv.astype(BF16)
        w = jnp.concatenate([wt[0], wt[1]], axis=1)
        lat_grad = dot(w, kv.T.astype(BF16)).astype(BF16)
        rope_grad = dk[:, 128:].T.astype(BF16)
        for e in range(2):
            dl[e, J, 0:512, :] = lat_grad[:, 128 * e : 128 * e + 128]
            dl[e, J, 512:576, :] = rope_grad[:, 128 * e : 128 * e + 128]
        remote(dl.at[1 - c, J], ra.at[J], ras.at[J], rar.at[J], other_core).start()

    def z_rows(base, size, zz):
        return pl.ds(pl.multiple_of(base + zz * size, 16), size)

    def add_cores(J):
        remote(ra.at[J], ra.at[J], ras.at[J], rar.at[J], other_core).wait_recv()
        sa[J] = (dl[c, J].astype(F32) + ra[J].astype(F32)).astype(BF16)
        for j, dz in enumerate((1, 3, 2)):
            zz = z_peer(dz)
            remote(
                sa.at[J, z_rows(0, PART_Z, zz)], rb.at[J, z], rbs.at[3 * J + j], rbr.at[4 * J + z], (s, h * 4 + zz)
            ).start()

        @pl.when(J != k)
        def _():
            remote(
                sa.at[J, pl.ds(ALONG_Z, REST)], ry.at[k], rys.at[J], ryr.at[k], (2 * J + c, f)
            ).start()

    def add_along_z(J):
        acc = sa[J, z_rows(0, PART_Z, z), :].astype(F32)
        for dz in (1, 3, 2):
            zz = z_peer(dz)
            remote(rb.at[J, zz], rb.at[J, zz], rbs.at[0], rbr.at[4 * J + zz], other_core).wait_recv()
            acc = acc + rb[J, zz].astype(F32)
        sb[J] = acc.astype(BF16)

    def tile_at(step):
        turn = step // 2
        dy = turn + (turn // 2) * (1 - 2 * (turn % 2))
        return ((y + dy) % 4) * 2 + (x + step) % 2

    def query_step(step, carry):
        tile = tile_at(step)
        for e in range(2):
            d = 2 * tile + e

            @pl.when(s != d)
            def _():
                remote(iq.at[d], iq.at[d], iqs.at[0], iqr.at[d], other_core).wait_recv()

        for I in range(TILES):

            @pl.when(tile == I)
            def _():
                query_tile(I)

        for e in range(2):
            d = 2 * tile + e

            @pl.when(s != d)
            def _():
                remote(so.at[d], ro.at[s], os.at[d], orr.at[s], (d, f)).start()

        return carry

    lax.fori_loop(0, TILES, query_step, 0)
    def key_step(step, carry):
        tile = tile_at(TILES - 1 - step)
        for J in range(TILES):

            @pl.when(tile == J)
            def _():
                backward_keys(J)

        key_grads(tile)

        @pl.when(step >= LAG)
        def _():
            add_cores(tile_at(TILES - 1 - step + LAG))

        @pl.when(step >= 2 * LAG)
        def _():
            add_along_z(tile_at(TILES - 1 - step + 2 * LAG))

        return carry

    lax.fori_loop(0, TILES, key_step, 0)
    w_grad = jnp.zeros((512, 256), F32)
    for t in range(TILES):
        w_grad = w_grad + dot(tile_of(lat, t, 0, 512), kvs[t])
    w_grad = w_grad.astype(BF16)
    for d in range(16):
        sdw[d, 0:32, :] = w_grad[32 * d : 32 * d + 32, :128]
        sdw[d, 32:64, :] = w_grad[32 * d : 32 * d + 32, 128:]
    for step in range(LAG - 1, -1, -1):
        add_cores(tile_at(step))
    for i, r in enumerate(SEQ_PEERS):
        p = seq_peer(r)
        cp = remote(sdw.at[p], rw.at[s], ws.at[i], wr.at[s], (p, f))
        cp.start()
        sends.append(cp)
    for step in range(2 * LAG - 1, -1, -1):
        add_along_z(tile_at(step))

    for i, r in enumerate(CHIP_PEERS):
        q = chip_peer(r)
        cp = remote(sb.at[q], rc.at[k], rcs.at[i], rcr.at[k], (2 * q + c, f))
        cp.start()
        sends.append(cp)
    acc = sa[k, ALONG_Z:576, :].astype(F32)
    for r in CHIP_PEERS:
        q = chip_peer(r)
        remote(ry.at[q], ry.at[q], rys.at[0], ryr.at[q], other_core).wait_recv()
        acc = acc + ry[q].astype(F32)
    sy[...] = acc.astype(BF16)
    for j, dz in enumerate((1, 3, 2)):
        zz = z_peer(dz)
        cp = remote(sy.at[z_rows(0, PART_REST, zz)], rz.at[z], rzs.at[j], rzr.at[z], (s, h * 4 + zz))
        cp.start()
        sends.append(cp)
    acc = sb[k].astype(F32)
    for r in CHIP_PEERS:
        q = chip_peer(r)
        remote(rc.at[q], rc.at[q], rcs.at[0], rcr.at[q], other_core).wait_recv()
        acc = acc + rc[q].astype(F32)
    part[0:PART_Z, :] = acc.astype(BF16)
    acc = sy[z_rows(0, PART_REST, z), :].astype(F32)
    for dz in (1, 3, 2):
        zz = z_peer(dz)
        remote(rz.at[zz], rz.at[zz], rzs.at[0], rzr.at[zz], other_core).wait_recv()
        acc = acc + rz[zz].astype(F32)
    part[PART_Z:PART, :] = acc.astype(BF16)
    cp = remote(part, other, hs.at[0], hr.at[0], (s, (1 - h) * 4 + z))
    cp.start()
    sends.append(cp)
    cp.wait_recv()
    whole[...] = (part[...].astype(F32) + other[...].astype(F32)).astype(BF16)
    for j, dz in enumerate((1, 3, 2)):
        cp = remote(whole, fe.at[z], es.at[j], er.at[z], (s, h * 4 + z_peer(dz)))
        cp.start()
        sends.append(cp)
    mine = [
        pltpu.make_async_copy(src, dst, own.at[i])
        for i, (src, dst) in enumerate(
            [(so.at[s], ro.at[s]), (sdw.at[s], rw.at[s]), (whole, fe.at[z])]
        )
    ]
    for cp in mine:
        cp.start()

    for r in SEQ_PEERS:
        p = seq_peer(r)
        remote(ro.at[p], ro.at[p], os.at[0], orr.at[p], other_core).wait_recv()
        remote(rw.at[p], rw.at[p], ws.at[0], wr.at[p], other_core).wait_recv()
        remote(so.at[p], so.at[p], os.at[p], orr.at[p], other_core).wait_send()
    for dz in (1, 3, 2):
        zz = z_peer(dz)
        remote(whole, fe.at[zz], es.at[0], er.at[zz], other_core).wait_recv()
    for cp in mine:
        cp.wait()
    for cp in sends:
        cp.wait_send()
    for J in range(TILES):
        remote(ra.at[J], ra.at[J], ras.at[J], rar.at[J], other_core).wait_send()
        for j in range(3):
            remote(rb.at[J, 0], rb.at[J, 0], rbs.at[3 * J + j], rbr.at[0], other_core).wait_send()

        @pl.when(J != k)
        def _():
            remote(ry.at[0], ry.at[0], rys.at[J], ryr.at[0], other_core).wait_send()


def unpack(
    ro_hbm, rw_hbm, fe_hbm, out, dqn, dqr, dlat, dkr, duk, duv, ro, rw, fe, sems
):
    loads = [
        pltpu.make_async_copy(src, dst, sems.at[i])
        for i, (src, dst) in enumerate([(ro_hbm, ro), (rw_hbm, rw), (fe_hbm, fe)])
    ]
    for cp in loads:
        cp.start()
    for cp in loads:
        cp.wait()
    for d in range(16):
        cols = slice(128 * d, 128 * d + 128)
        out[:, cols] = ro[d, 0:128, :]
        dqn[:, cols] = ro[d, 128:256, :]
        duk[:, cols] = rw[d, 0:32, :].astype(F32)
        duv[:, cols] = rw[d, 32:64, :].astype(F32)
    for pair in range(8):
        both = [unpack_rope(ro[2 * pair + e, 256:320, :].astype(F32)) for e in range(2)]
        dqr[:, 128 * pair : 128 * pair + 128] = jnp.concatenate(both, axis=1).astype(BF16)
    for z in range(4):
        dlat[PART_Z * z : PART_Z * z + PART_Z, :] = fe[z, 0:PART_Z, :]
        rest = fe[z, PART_Z:PART, :]
        lo = ALONG_Z + PART_REST * z
        if lo < 512:
            dlat[lo : lo + PART_REST, :] = rest
        else:
            dkr[lo - 512 : lo - 512 + PART_REST, :] = rest


def on_device(q_nope, q_rope, latent_t, k_rope_t, w_uk, w_uv, grad_out, seg_ids, anc_flags):
    vmem = pl.BlockSpec(memory_space=pltpu.VMEM)
    smem = pl.BlockSpec(memory_space=pltpu.SMEM)
    anywhere = pl.BlockSpec(memory_space=pl.ANY)
    dma = pltpu.SemaphoreType.DMA
    sem_counts = [7, 3, 7, 8, 21, 32, 8, 8, 15, 16, 15, 16, 16, 16, 8, 8, 24, 32, 7, 8]
    sem_counts += [8, 8, 3, 4, 1, 1, 15, 16, 3, 4]
    parts = pl.pallas_call(
        fused,
        out_shape=[
            jax.ShapeDtypeStruct((16, 320, 128), BF16),
            jax.ShapeDtypeStruct((16, 64, 128), BF16),
            jax.ShapeDtypeStruct((4, PART, 128), BF16),
        ],
        in_specs=[smem, smem] + [anywhere] * 7,
        out_specs=[anywhere] * 3,
        scratch_shapes=[
            pltpu.VMEM((128, 2048), BF16),
            pltpu.VMEM((128, 1024), BF16),
            pltpu.VMEM((32, 2048), BF16),
            pltpu.VMEM((32, 2048), BF16),
            pltpu.VMEM((128, 2048), BF16),
            pltpu.VMEM((2, 8, 576, 128), BF16),
            pltpu.VMEM((16, 64, 128), BF16),
            pltpu.VMEM((16, 64, 128), BF16),
            pltpu.VMEM((16, 320, 128), BF16),
            pltpu.VMEM((16, 320, 128), BF16),
            pltpu.VMEM((2, 512, 128), BF16),
            pltpu.VMEM((256, 512), BF16),
            pltpu.VMEM((8, 192, 256), BF16),
            pltpu.VMEM((8, 128, 256), BF16),
            pltpu.VMEM((8, 256, 192), BF16),
            pltpu.VMEM((8, 256, 128), BF16),
            pltpu.VMEM((8, 256, 256), F32),
            pltpu.VMEM((36, 256, 256), BF16),
            pltpu.VMEM((36, 256, 256), BF16),
            pltpu.VMEM((8, 256, 192), BF16),
            pltpu.VMEM((8, 256, 128), BF16),
            pltpu.VMEM((256, 192), F32),
            pltpu.VMEM((256, 128), F32),
            pltpu.VMEM((8, 256, 256), BF16),
            pltpu.VMEM((16, 320, 128), BF16),
            pltpu.VMEM((16, 64, 128), BF16),
            pltpu.VMEM((2, 8, 576, 128), BF16),
            pltpu.VMEM((8, 576, 128), BF16),
            pltpu.VMEM((8, 576, 128), BF16),
            pltpu.VMEM((8, 4, PART_Z, 128), BF16),
            pltpu.VMEM((8, PART_Z, 128), BF16),
            pltpu.VMEM((8, PART_Z, 128), BF16),
            pltpu.VMEM((8, REST, 128), BF16),
            pltpu.VMEM((REST, 128), BF16),
            pltpu.VMEM((4, PART_REST, 128), BF16),
            pltpu.VMEM((PART, 128), BF16),
            pltpu.VMEM((PART, 128), BF16),
            pltpu.VMEM((PART, 128), BF16),
        ]
        + [dma((n,)) for n in sem_counts],
        compiler_params=pltpu.CompilerParams(
            collective_id=0, has_side_effects=True, vmem_limit_bytes=56 * 1024 * 1024
        ),
        name="attention_exchange",
    )(seg_ids, anc_flags, q_nope, q_rope, latent_t, k_rope_t, w_uk, w_uv, grad_out)
    bf, fl = BF16, F32
    return pl.pallas_call(
        unpack,
        out_shape=[
            jax.ShapeDtypeStruct((128, 2048), bf),
            jax.ShapeDtypeStruct((128, 2048), bf),
            jax.ShapeDtypeStruct((128, 1024), bf),
            jax.ShapeDtypeStruct((512, 128), bf),
            jax.ShapeDtypeStruct((64, 128), bf),
            jax.ShapeDtypeStruct((32, 2048), fl),
            jax.ShapeDtypeStruct((32, 2048), fl),
        ],
        in_specs=[anywhere] * 3,
        out_specs=[vmem] * 7,
        scratch_shapes=[
            pltpu.VMEM((16, 320, 128), bf),
            pltpu.VMEM((16, 64, 128), bf),
            pltpu.VMEM((4, PART, 128), bf),
            dma((3,)),
        ],
        compiler_params=pltpu.CompilerParams(vmem_limit_bytes=60 * 1024 * 1024),
        name="unpack",
    )(*parts)


def solution(mesh):
    placed = (
        P("seq", "fsdp"),
        P("seq", "fsdp"),
        P(None, "seq"),
        P(None, "seq"),
        P("seq", "fsdp"),
        P("seq", "fsdp"),
        P("seq", "fsdp"),
        P(),
        P(),
    )
    return jax.shard_map(
        on_device,
        mesh=mesh,
        in_specs=placed,
        out_specs=(
            P("seq", "fsdp"),
            P("seq", "fsdp"),
            P("seq", "fsdp"),
            P(None, "seq"),
            P(None, "seq"),
            P("seq", "fsdp"),
            P("seq", "fsdp"),
        ),
        check_vma=False,
    )
```

```python
import functools
import math

import jax
import jax.numpy as jnp
from jax import lax
from jax.experimental import pallas as pl
from jax.experimental.pallas import tpu as pltpu
from jax.sharding import PartitionSpec as P

F32, BF16 = jnp.float32, jnp.bfloat16
MESH = pl.DeviceIdType.MESH
NEG = -1e30
SCALE = 1.0 / math.sqrt(192.0)
SCALE_LOG2E = SCALE * math.log2(math.e)
TILES = 8
LAG = 3
LAT_Z = 512
LAT_PART = LAT_Z // 4
PART = 144
ALONG_Z = 320
PART_Z = ALONG_Z // 4
REST = 576 - ALONG_Z
PART_REST = REST // 4

SEQ_PEERS = [(dy, dx, dc) for dy in (0, 3, 1, 2) for dx in (0, 1) for dc in (0, 1)][1:]
CHIP_PEERS = [(0, 1), (1, 0), (3, 0), (2, 0), (1, 1), (3, 1), (2, 1)]


def dot(left, right):
    return lax.dot_general(left, right, (((1,), (0,)), ((), ())), preferred_element_type=F32)


def unpack_rope(x):
    return jnp.concatenate([x[:, :64], x[:, 64:]], axis=0)


def pack_rope(x):
    return jnp.concatenate([x[:64], x[64:]], axis=1)


def tile_of(lat, t, lo, hi):
    return jnp.concatenate([lat[0, t, lo:hi, :], lat[1, t, lo:hi, :]], axis=1)


def fused(
    seg, anc, qn_hbm, qr_hbm, lt_hbm, kr_hbm, uk_hbm, uv_hbm, g_hbm,
    ro, rw, fe,
    qn_in, qr_in, uk_in, uv_in, g_in,
    lat, sw, iw, sq, iq, wt, wtT, kcT, vT, kc, v, sc, dss, ps, qcs, gcs, dks, dvs, kvs, so, sdw, dl, ra, sa,
    rb, sb, rc, ry, sy, rz, part, other, whole,
    ins, own, l1s, l1r, lds, ldr, l2s, l2r, l3s, l3r, iws, iwr, iqs, iqr, os, orr, ras, rar, rbs, rbr, rcs, rcr,
    rys, ryr, rzs, rzr, hs, hr, ws, wr, es, er,
):
    s, f = lax.axis_index("seq"), lax.axis_index("fsdp")
    y, x, c = s // 4, (s // 2) % 2, s % 2
    k = s // 2
    h, z = f // 4, f % 4

    def seq_peer(rel):
        return ((y + rel[0]) % 4) * 4 + ((x + rel[1]) % 2) * 2 + (c + rel[2]) % 2

    def chip_peer(rel):
        return ((y + rel[0]) % 4) * 2 + (x + rel[1]) % 2

    def z_peer(dz):
        return (z + dz) % 4

    other_core = (k * 2 + 1 - c, f)
    zrow = pl.multiple_of(z * LAT_PART, 16)

    def remote(src, dst, ssem, rsem, device):
        return pltpu.make_async_remote_copy(
            src_ref=src, dst_ref=dst, send_sem=ssem, recv_sem=rsem, device_id=device, device_id_type=MESH
        )

    loads = [
        pltpu.make_async_copy(src, dst, ins.at[i])
        for i, (src, dst) in enumerate(
            [
                (lt_hbm, lat.at[c, k, pl.ds(0, 512)]),
                (kr_hbm, lat.at[c, k, pl.ds(512, 64)]),
                (uk_hbm, uk_in),
                (uv_hbm, uv_in),
                (qn_hbm, qn_in),
                (qr_hbm, qr_in),
                (g_hbm, g_in),
            ]
        )
    ]
    for cp in loads:
        cp.start()

    bar = pltpu.get_barrier_semaphore()
    peers = [(seq_peer(r), f) for r in SEQ_PEERS]
    peers += [(s, h * 4 + z_peer(dz)) for dz in (1, 2, 3)]
    peers += [(s, (1 - h) * 4 + z)]
    for p in peers:
        pl.semaphore_signal(bar, inc=1, device_id=p, device_id_type=MESH)

    for cp in loads:
        cp.wait()
    for d in range(16):
        sw[d, 0:32, :] = uk_in[:, 128 * d : 128 * d + 128]
        sw[d, 32:64, :] = uv_in[:, 128 * d : 128 * d + 128]
        sq[d, 0:128, :] = qn_in[:, 128 * d : 128 * d + 128]
        sq[d, 192:320, :] = g_in[:, 128 * d : 128 * d + 128]
    for pair in range(8):
        both = qr_in[:, 128 * pair : 128 * pair + 128].astype(F32)
        sq[2 * pair, 128:192, :] = pack_rope(both[:, :64]).astype(BF16)
        sq[2 * pair + 1, 128:192, :] = pack_rope(both[:, 64:]).astype(BF16)
    iw[s] = sw[s]
    iq[s] = sq[s]
    pl.semaphore_wait(bar, len(peers))

    sends = []

    mine = lat.at[c, k, pl.ds(zrow, LAT_PART)]
    rest = lat.at[c, k, pl.ds(LAT_Z, 576 - LAT_Z)]
    for i, r in enumerate(CHIP_PEERS):
        cp = remote(mine, mine, l1s.at[i], l1r.at[k], (chip_peer(r) * 2 + c, f))
        cp.start()
        sends.append(cp)
    for i, r in enumerate(CHIP_PEERS):
        cp = remote(rest, rest, lds.at[i], ldr.at[k], (chip_peer(r) * 2 + c, f))
        cp.start()
        sends.append(cp)
    cp = remote(lat.at[c, k], lat.at[c, k], l3s.at[k], l3r.at[k], other_core)
    cp.start()
    sends.append(cp)
    for i, r in enumerate(SEQ_PEERS):
        p = seq_peer(r)
        cp = remote(sw.at[p], iw.at[s], iws.at[i], iwr.at[s], (p, f))
        cp.start()
        sends.append(cp)
    for i, r in enumerate(CHIP_PEERS):
        q = chip_peer(r)
        piece = lat.at[c, q, pl.ds(zrow, LAT_PART)]
        remote(piece, piece, l1s.at[i], l1r.at[q], other_core).wait_recv()
        for j, dz in enumerate((1, 3, 2)):
            cp = remote(piece, piece, l2s.at[3 * i + j], l2r.at[4 * q + z], (s, h * 4 + z_peer(dz)))
            cp.start()
            sends.append(cp)
    for r in CHIP_PEERS:
        block = lat.at[c, chip_peer(r), pl.ds(LAT_Z, 576 - LAT_Z)]
        remote(block, block, lds.at[0], ldr.at[chip_peer(r)], other_core).wait_recv()
    for r in SEQ_PEERS:
        p = seq_peer(r)
        remote(iw.at[p], iw.at[p], iws.at[0], iwr.at[p], other_core).wait_recv()

    def send_queries(peers):
        for i in peers:
            for e in range(2):
                p = chip_peer(CHIP_PEERS[i]) * 2 + e
                remote(sq.at[p], iq.at[s], iqs.at[2 * i + e], iqr.at[s], (p, f)).start()

    remote(sq.at[k * 2 + 1 - c], iq.at[s], iqs.at[14], iqr.at[s], other_core).start()
    send_queries(range(7))
    for d in range(16):
        wt[0, 32 * d : 32 * d + 32, :] = iw[d, 0:32, :]
        wt[1, 32 * d : 32 * d + 32, :] = iw[d, 32:64, :]
    wtT[0:128, :] = wt[0].astype(F32).T.astype(BF16)
    wtT[128:256, :] = wt[1].astype(F32).T.astype(BF16)

    for i, r in enumerate(CHIP_PEERS):
        q = chip_peer(r)
        for dz in (1, 3, 2):
            zz = z_peer(dz)
            piece = lat.at[c, q, pl.ds(pl.multiple_of(zz * LAT_PART, 16), LAT_PART)]
            remote(piece, piece, l2s.at[0], l2r.at[4 * q + zz], other_core).wait_recv()
        cp = remote(lat.at[c, q], lat.at[c, q], l3s.at[q], l3r.at[q], other_core)
        cp.start()
        sends.append(cp)


    for r in [(0, 0)] + CHIP_PEERS:
        t = chip_peer(r)
        block = lat.at[1 - c, t]
        remote(block, block, l3s.at[0], l3r.at[t], other_core).wait_recv()
        rope = tile_of(lat, t, 512, 576)
        kv = dot(wtT[...], tile_of(lat, t, 0, 512))
        kcT[t, 0:128, :] = kv[:128].astype(BF16)
        kcT[t, 128:192, :] = rope
        vT[t] = kv[128:].astype(BF16)
        kc[t, :, 0:128] = kv[:128].T.astype(BF16)
        kc[t, :, 128:192] = rope.astype(F32).T.astype(BF16)
        v[t] = kv[128:].T.astype(BF16)

    lane = lax.broadcasted_iota(jnp.int32, (1, 256), 1)

    def bias_of(a, b):
        seen = (seg[128 * a] == seg[128 * b]) | (anc[a, b] == 1)
        return jnp.where(seen, 0.0, NEG).astype(F32)

    def pair_index(I, J):
        return I * (I + 1) // 2 + J

    def query_tile(I):
        a0, a1 = iq[2 * I], iq[2 * I + 1]
        qn = jnp.concatenate([a0[0:128], a1[0:128]], axis=0)
        g = jnp.concatenate([a0[192:320], a1[192:320]], axis=0)
        qr = jnp.concatenate(
            [unpack_rope(a0[128:192].astype(F32)), unpack_rope(a1[128:192].astype(F32))], axis=0
        )
        qT = jnp.concatenate([qn.astype(F32).T, qr.T], axis=0).astype(BF16)
        qcs[I] = jnp.concatenate([qn, qr.astype(BF16)], axis=1)
        gcs[I] = g
        gT = g.astype(F32).T
        top = jnp.full((1, 256), NEG, F32)
        for J in range(I + 1):
            scores = dot(kc[J], qT)
            if J < I:
                halves = []
                for b in range(2):
                    bias = jnp.where(
                        lane < 128, bias_of(2 * I, 2 * J + b), bias_of(2 * I + 1, 2 * J + b)
                    )
                    halves.append(scores[128 * b : 128 * b + 128] + bias)
                scores = jnp.concatenate(halves, axis=0)
            else:
                key = lax.broadcasted_iota(jnp.int32, (256, 256), 0)
                query = lax.broadcasted_iota(jnp.int32, (256, 256), 1)
                bias = jnp.where(lane < 128, 0.0, bias_of(2 * I + 1, 2 * I))
                scores = jnp.concatenate([scores[:128] + bias, scores[128:]], axis=0)
                scores = jnp.where(key <= query, scores, NEG)
            sc[J] = scores
            top = jnp.maximum(top, jnp.max(scores, axis=0, keepdims=True))
        top = top * SCALE_LOG2E
        total = jnp.zeros((1, 256), F32)
        oT = jnp.zeros((128, 256), F32)
        for J in range(I + 1):
            weight = jnp.exp2(sc[J] * SCALE_LOG2E - top)
            total = total + jnp.sum(weight, axis=0, keepdims=True)
            sc[J] = weight
            oT = oT + dot(vT[J], weight.astype(BF16))
        inverse = 1.0 / total
        oT = oT * inverse
        delta = jnp.sum(oT * gT, axis=0, keepdims=True)
        gT = gT.astype(BF16)
        dqT = jnp.zeros((192, 256), F32)
        for J in range(I + 1):
            prob = sc[J] * inverse
            ds = (prob * (dot(v[J], gT) - delta)).astype(BF16)
            dss[pair_index(I, J)] = ds
            ps[pair_index(I, J)] = prob.astype(BF16)
            dqT = dqT + dot(kcT[J], ds)
        dqT = dqT * SCALE
        o = oT.T.astype(BF16)
        dqn = dqT[:128].T.astype(BF16)
        dqr = dqT[128:].T
        for e in range(2):
            lo = 128 * e
            so[2 * I + e, 0:128, :] = o[lo : lo + 128]
            so[2 * I + e, 128:256, :] = dqn[lo : lo + 128]
            so[2 * I + e, 256:320, :] = pack_rope(dqr[lo : lo + 128]).astype(BF16)

    def backward_keys(J):
        dk = jnp.zeros((256, 192), F32)
        dv = jnp.zeros((256, 128), F32)
        for I in range(J, TILES):
            dk = dk + dot(dss[pair_index(I, J)], qcs[I])
            dv = dv + dot(ps[pair_index(I, J)], gcs[I])
        dk = dk * SCALE
        dks[...] = dk
        dvs[...] = dv

    def key_grads(J):
        dk = dks[...]
        kv = jnp.concatenate([dk[:, :128], dvs[...]], axis=1)
        kvs[J] = kv.astype(BF16)
        w = jnp.concatenate([wt[0], wt[1]], axis=1)
        lat_grad = dot(w, kv.T.astype(BF16)).astype(BF16)
        rope_grad = dk[:, 128:].T.astype(BF16)
        for e in range(2):
            dl[e, J, 0:512, :] = lat_grad[:, 128 * e : 128 * e + 128]
            dl[e, J, 512:576, :] = rope_grad[:, 128 * e : 128 * e + 128]
        remote(dl.at[1 - c, J], ra.at[J], ras.at[J], rar.at[J], other_core).start()

    def z_rows(base, size, zz):
        return pl.ds(pl.multiple_of(base + zz * size, 16), size)

    def add_cores(J):
        remote(ra.at[J], ra.at[J], ras.at[J], rar.at[J], other_core).wait_recv()
        sa[J] = (dl[c, J].astype(F32) + ra[J].astype(F32)).astype(BF16)
        for j, dz in enumerate((1, 3, 2)):
            zz = z_peer(dz)
            remote(
                sa.at[J, z_rows(0, PART_Z, zz)], rb.at[J, z], rbs.at[3 * J + j], rbr.at[4 * J + z], (s, h * 4 + zz)
            ).start()

        @pl.when(J != k)
        def _():
            remote(
                sa.at[J, pl.ds(ALONG_Z, REST)], ry.at[k], rys.at[J], ryr.at[k], (2 * J + c, f)
            ).start()

    def add_along_z(J):
        acc = sa[J, z_rows(0, PART_Z, z), :].astype(F32)
        for dz in (1, 3, 2):
            zz = z_peer(dz)
            remote(rb.at[J, zz], rb.at[J, zz], rbs.at[0], rbr.at[4 * J + zz], other_core).wait_recv()
            acc = acc + rb[J, zz].astype(F32)
        sb[J] = acc.astype(BF16)

    def tile_at(step):
        far = (step + 6) // 8
        turn = (step + 1) % 3
        dy = far * (1 + 2 * turn - 3 * (turn // 2))
        dx = (1 - far) * step + far * ((step + 1) // 3 - 1)
        return ((y + dy) % 4) * 2 + (x + dx) % 2

    def query_step(step, carry):
        tile = tile_at(step)
        for e in range(2):
            d = 2 * tile + e

            @pl.when(s != d)
            def _():
                remote(iq.at[d], iq.at[d], iqs.at[0], iqr.at[d], other_core).wait_recv()

        for I in range(TILES):

            @pl.when(tile == I)
            def _():
                query_tile(I)

        for e in range(2):
            d = 2 * tile + e

            @pl.when(s != d)
            def _():
                remote(so.at[d], ro.at[s], os.at[d], orr.at[s], (d, f)).start()

        return carry

    lax.fori_loop(0, TILES, query_step, 0)
    def key_step(step, carry):
        tile = tile_at(TILES - 1 - step)
        for J in range(TILES):

            @pl.when(tile == J)
            def _():
                backward_keys(J)

        key_grads(tile)

        @pl.when(step >= LAG)
        def _():
            add_cores(tile_at(TILES - 1 - step + LAG))

        @pl.when(step >= 2 * LAG)
        def _():
            add_along_z(tile_at(TILES - 1 - step + 2 * LAG))

        return carry

    lax.fori_loop(0, TILES, key_step, 0)
    w_grad = jnp.zeros((512, 256), F32)
    for t in range(TILES):
        w_grad = w_grad + dot(tile_of(lat, t, 0, 512), kvs[t])
    w_grad = w_grad.astype(BF16)
    for d in range(16):
        sdw[d, 0:32, :] = w_grad[32 * d : 32 * d + 32, :128]
        sdw[d, 32:64, :] = w_grad[32 * d : 32 * d + 32, 128:]
    for step in range(LAG - 1, -1, -1):
        add_cores(tile_at(step))
    for i, r in enumerate(SEQ_PEERS):
        p = seq_peer(r)
        cp = remote(sdw.at[p], rw.at[s], ws.at[i], wr.at[s], (p, f))
        cp.start()
        sends.append(cp)
    for step in range(2 * LAG - 1, -1, -1):
        add_along_z(tile_at(step))

    for i, r in enumerate(CHIP_PEERS):
        q = chip_peer(r)
        cp = remote(sb.at[q], rc.at[k], rcs.at[i], rcr.at[k], (2 * q + c, f))
        cp.start()
        sends.append(cp)
    acc = sa[k, ALONG_Z:576, :].astype(F32)
    for r in CHIP_PEERS:
        q = chip_peer(r)
        remote(ry.at[q], ry.at[q], rys.at[0], ryr.at[q], other_core).wait_recv()
        acc = acc + ry[q].astype(F32)
    sy[...] = acc.astype(BF16)
    for j, dz in enumerate((1, 3, 2)):
        zz = z_peer(dz)
        cp = remote(sy.at[z_rows(0, PART_REST, zz)], rz.at[z], rzs.at[j], rzr.at[z], (s, h * 4 + zz))
        cp.start()
        sends.append(cp)
    acc = sb[k].astype(F32)
    for r in CHIP_PEERS:
        q = chip_peer(r)
        remote(rc.at[q], rc.at[q], rcs.at[0], rcr.at[q], other_core).wait_recv()
        acc = acc + rc[q].astype(F32)
    part[0:PART_Z, :] = acc.astype(BF16)
    acc = sy[z_rows(0, PART_REST, z), :].astype(F32)
    for dz in (1, 3, 2):
        zz = z_peer(dz)
        remote(rz.at[zz], rz.at[zz], rzs.at[0], rzr.at[zz], other_core).wait_recv()
        acc = acc + rz[zz].astype(F32)
    part[PART_Z:PART, :] = acc.astype(BF16)
    cp = remote(part, other, hs.at[0], hr.at[0], (s, (1 - h) * 4 + z))
    cp.start()
    sends.append(cp)
    cp.wait_recv()
    whole[...] = (part[...].astype(F32) + other[...].astype(F32)).astype(BF16)
    for j, dz in enumerate((1, 3, 2)):
        cp = remote(whole, fe.at[z], es.at[j], er.at[z], (s, h * 4 + z_peer(dz)))
        cp.start()
        sends.append(cp)
    kept = [
        pltpu.make_async_copy(src, dst, own.at[i])
        for i, (src, dst) in enumerate(
            [(so.at[s], ro.at[s]), (sdw.at[s], rw.at[s]), (whole, fe.at[z])]
        )
    ]
    for cp in kept:
        cp.start()

    for r in SEQ_PEERS:
        p = seq_peer(r)
        remote(ro.at[p], ro.at[p], os.at[0], orr.at[p], other_core).wait_recv()
        remote(rw.at[p], rw.at[p], ws.at[0], wr.at[p], other_core).wait_recv()
        remote(so.at[p], so.at[p], os.at[p], orr.at[p], other_core).wait_send()
    for dz in (1, 3, 2):
        zz = z_peer(dz)
        remote(whole, fe.at[zz], es.at[0], er.at[zz], other_core).wait_recv()
    for cp in kept:
        cp.wait()
    for cp in sends:
        cp.wait_send()
    for i in range(15):
        remote(sq.at[0], sq.at[0], iqs.at[i], iqr.at[0], other_core).wait_send()
    for J in range(TILES):
        remote(ra.at[J], ra.at[J], ras.at[J], rar.at[J], other_core).wait_send()
        for j in range(3):
            remote(rb.at[J, 0], rb.at[J, 0], rbs.at[3 * J + j], rbr.at[0], other_core).wait_send()

        @pl.when(J != k)
        def _():
            remote(ry.at[0], ry.at[0], rys.at[J], ryr.at[0], other_core).wait_send()


def unpack(
    ro_hbm, rw_hbm, fe_hbm, out, dqn, dqr, dlat, dkr, duk, duv, ro, rw, fe, sems
):
    loads = [
        pltpu.make_async_copy(src, dst, sems.at[i])
        for i, (src, dst) in enumerate([(ro_hbm, ro), (rw_hbm, rw), (fe_hbm, fe)])
    ]
    for cp in loads:
        cp.start()
    for cp in loads:
        cp.wait()
    for d in range(16):
        cols = slice(128 * d, 128 * d + 128)
        out[:, cols] = ro[d, 0:128, :]
        dqn[:, cols] = ro[d, 128:256, :]
        duk[:, cols] = rw[d, 0:32, :].astype(F32)
        duv[:, cols] = rw[d, 32:64, :].astype(F32)
    for pair in range(8):
        both = [unpack_rope(ro[2 * pair + e, 256:320, :].astype(F32)) for e in range(2)]
        dqr[:, 128 * pair : 128 * pair + 128] = jnp.concatenate(both, axis=1).astype(BF16)
    for z in range(4):
        dlat[PART_Z * z : PART_Z * z + PART_Z, :] = fe[z, 0:PART_Z, :]
        rest = fe[z, PART_Z:PART, :]
        lo = ALONG_Z + PART_REST * z
        if lo < 512:
            dlat[lo : lo + PART_REST, :] = rest
        else:
            dkr[lo - 512 : lo - 512 + PART_REST, :] = rest


def on_device(q_nope, q_rope, latent_t, k_rope_t, w_uk, w_uv, grad_out, seg_ids, anc_flags):
    vmem = pl.BlockSpec(memory_space=pltpu.VMEM)
    smem = pl.BlockSpec(memory_space=pltpu.SMEM)
    anywhere = pl.BlockSpec(memory_space=pl.ANY)
    dma = pltpu.SemaphoreType.DMA
    sem_counts = [7, 3, 7, 8, 7, 8, 21, 32, 8, 8, 15, 16, 15, 16, 16, 16, 8, 8, 24, 32, 7, 8]
    sem_counts += [8, 8, 3, 4, 1, 1, 15, 16, 3, 4]
    parts = pl.pallas_call(
        fused,
        out_shape=[
            jax.ShapeDtypeStruct((16, 320, 128), BF16),
            jax.ShapeDtypeStruct((16, 64, 128), BF16),
            jax.ShapeDtypeStruct((4, PART, 128), BF16),
        ],
        in_specs=[smem, smem] + [anywhere] * 7,
        out_specs=[anywhere] * 3,
        scratch_shapes=[
            pltpu.VMEM((128, 2048), BF16),
            pltpu.VMEM((128, 1024), BF16),
            pltpu.VMEM((32, 2048), BF16),
            pltpu.VMEM((32, 2048), BF16),
            pltpu.VMEM((128, 2048), BF16),
            pltpu.VMEM((2, 8, 576, 128), BF16),
            pltpu.VMEM((16, 64, 128), BF16),
            pltpu.VMEM((16, 64, 128), BF16),
            pltpu.VMEM((16, 320, 128), BF16),
            pltpu.VMEM((16, 320, 128), BF16),
            pltpu.VMEM((2, 512, 128), BF16),
            pltpu.VMEM((256, 512), BF16),
            pltpu.VMEM((8, 192, 256), BF16),
            pltpu.VMEM((8, 128, 256), BF16),
            pltpu.VMEM((8, 256, 192), BF16),
            pltpu.VMEM((8, 256, 128), BF16),
            pltpu.VMEM((8, 256, 256), F32),
            pltpu.VMEM((36, 256, 256), BF16),
            pltpu.VMEM((36, 256, 256), BF16),
            pltpu.VMEM((8, 256, 192), BF16),
            pltpu.VMEM((8, 256, 128), BF16),
            pltpu.VMEM((256, 192), F32),
            pltpu.VMEM((256, 128), F32),
            pltpu.VMEM((8, 256, 256), BF16),
            pltpu.VMEM((16, 320, 128), BF16),
            pltpu.VMEM((16, 64, 128), BF16),
            pltpu.VMEM((2, 8, 576, 128), BF16),
            pltpu.VMEM((8, 576, 128), BF16),
            pltpu.VMEM((8, 576, 128), BF16),
            pltpu.VMEM((8, 4, PART_Z, 128), BF16),
            pltpu.VMEM((8, PART_Z, 128), BF16),
            pltpu.VMEM((8, PART_Z, 128), BF16),
            pltpu.VMEM((8, REST, 128), BF16),
            pltpu.VMEM((REST, 128), BF16),
            pltpu.VMEM((4, PART_REST, 128), BF16),
            pltpu.VMEM((PART, 128), BF16),
            pltpu.VMEM((PART, 128), BF16),
            pltpu.VMEM((PART, 128), BF16),
        ]
        + [dma((n,)) for n in sem_counts],
        compiler_params=pltpu.CompilerParams(
            collective_id=0, has_side_effects=True, vmem_limit_bytes=56 * 1024 * 1024
        ),
        name="attention_exchange",
    )(seg_ids, anc_flags, q_nope, q_rope, latent_t, k_rope_t, w_uk, w_uv, grad_out)
    bf, fl = BF16, F32
    return pl.pallas_call(
        unpack,
        out_shape=[
            jax.ShapeDtypeStruct((128, 2048), bf),
            jax.ShapeDtypeStruct((128, 2048), bf),
            jax.ShapeDtypeStruct((128, 1024), bf),
            jax.ShapeDtypeStruct((512, 128), bf),
            jax.ShapeDtypeStruct((64, 128), bf),
            jax.ShapeDtypeStruct((32, 2048), fl),
            jax.ShapeDtypeStruct((32, 2048), fl),
        ],
        in_specs=[anywhere] * 3,
        out_specs=[vmem] * 7,
        scratch_shapes=[
            pltpu.VMEM((16, 320, 128), bf),
            pltpu.VMEM((16, 64, 128), bf),
            pltpu.VMEM((4, PART, 128), bf),
            dma((3,)),
        ],
        compiler_params=pltpu.CompilerParams(vmem_limit_bytes=60 * 1024 * 1024),
        name="unpack",
    )(*parts)


def solution(mesh):
    placed = (
        P("seq", "fsdp"),
        P("seq", "fsdp"),
        P(None, "seq"),
        P(None, "seq"),
        P("seq", "fsdp"),
        P("seq", "fsdp"),
        P("seq", "fsdp"),
        P(),
        P(),
    )
    return jax.shard_map(
        on_device,
        mesh=mesh,
        in_specs=placed,
        out_specs=(
            P("seq", "fsdp"),
            P("seq", "fsdp"),
            P("seq", "fsdp"),
            P(None, "seq"),
            P(None, "seq"),
            P("seq", "fsdp"),
            P("seq", "fsdp"),
        ),
        check_vma=False,
    )
```

```python
import functools
import math

import jax
import jax.numpy as jnp
from jax import lax
from jax.experimental import pallas as pl
from jax.experimental.pallas import tpu as pltpu
from jax.sharding import PartitionSpec as P

F32, BF16 = jnp.float32, jnp.bfloat16
MESH = pl.DeviceIdType.MESH
NEG = -1e30
SCALE = 1.0 / math.sqrt(192.0)
SCALE_LOG2E = SCALE * math.log2(math.e)
TILES = 8
LAG = 3
LAT_Z = 512
LAT_PART = LAT_Z // 4
PART = 144
ALONG_Z = 320
PART_Z = ALONG_Z // 4
REST = 576 - ALONG_Z
PART_REST = REST // 4

SEQ_PEERS = [(dy, dx, dc) for dy in (0, 3, 1, 2) for dx in (0, 1) for dc in (0, 1)][1:]
CHIP_PEERS = [(0, 1), (1, 0), (3, 0), (2, 0), (1, 1), (3, 1), (2, 1)]


def dot(left, right):
    return lax.dot_general(left, right, (((1,), (0,)), ((), ())), preferred_element_type=F32)


def unpack_rope(x):
    return jnp.concatenate([x[:, :64], x[:, 64:]], axis=0)


def pack_rope(x):
    return jnp.concatenate([x[:64], x[64:]], axis=1)


def tile_of(lat, t, lo, hi):
    return jnp.concatenate([lat[0, t, lo:hi, :], lat[1, t, lo:hi, :]], axis=1)


def fused(
    seg, anc, qn_hbm, qr_hbm, lt_hbm, kr_hbm, uk_hbm, uv_hbm, g_hbm,
    ro, rw, fe,
    qn_in, qr_in, uk_in, uv_in, g_in,
    lat, sw, iw, sq, iq, wt, wtT, kcT, vT, kc, v, sc, dss, ps, qcs, gcs, dks, dvs, kvs, so, sdw, dl, ra, sa,
    rb, sb, rc, ry, sy, rz, part, other, whole,
    ins, own, l1s, l1r, lds, ldr, l2s, l2r, l3s, l3r, iws, iwr, iqs, iqr, os, orr, ras, rar, rbs, rbr, rcs, rcr,
    rys, ryr, rzs, rzr, hs, hr, ws, wr, es, er,
):
    s, f = lax.axis_index("seq"), lax.axis_index("fsdp")
    y, x, c = s // 4, (s // 2) % 2, s % 2
    k = s // 2
    h, z = f // 4, f % 4

    def seq_peer(rel):
        return ((y + rel[0]) % 4) * 4 + ((x + rel[1]) % 2) * 2 + (c + rel[2]) % 2

    def chip_peer(rel):
        return ((y + rel[0]) % 4) * 2 + (x + rel[1]) % 2

    def z_peer(dz):
        return (z + dz) % 4

    other_core = (k * 2 + 1 - c, f)
    zrow = pl.multiple_of(z * LAT_PART, 16)

    def remote(src, dst, ssem, rsem, device):
        return pltpu.make_async_remote_copy(
            src_ref=src, dst_ref=dst, send_sem=ssem, recv_sem=rsem, device_id=device, device_id_type=MESH
        )

    loads = [
        pltpu.make_async_copy(src, dst, ins.at[i])
        for i, (src, dst) in enumerate(
            [
                (lt_hbm, lat.at[c, k, pl.ds(0, 512)]),
                (kr_hbm, lat.at[c, k, pl.ds(512, 64)]),
                (uk_hbm, uk_in),
                (uv_hbm, uv_in),
                (qn_hbm, qn_in),
                (qr_hbm, qr_in),
                (g_hbm, g_in),
            ]
        )
    ]
    for cp in loads:
        cp.start()

    bar = pltpu.get_barrier_semaphore()
    peers = [(seq_peer(r), f) for r in SEQ_PEERS]
    peers += [(s, h * 4 + z_peer(dz)) for dz in (1, 2, 3)]
    peers += [(s, (1 - h) * 4 + z)]
    for p in peers:
        pl.semaphore_signal(bar, inc=1, device_id=p, device_id_type=MESH)

    for cp in loads:
        cp.wait()
    for d in range(16):
        sw[d, 0:32, :] = uk_in[:, 128 * d : 128 * d + 128]
        sw[d, 32:64, :] = uv_in[:, 128 * d : 128 * d + 128]
        sq[d, 0:128, :] = qn_in[:, 128 * d : 128 * d + 128]
        sq[d, 192:320, :] = g_in[:, 128 * d : 128 * d + 128]
    for pair in range(8):
        both = qr_in[:, 128 * pair : 128 * pair + 128].astype(F32)
        sq[2 * pair, 128:192, :] = pack_rope(both[:, :64]).astype(BF16)
        sq[2 * pair + 1, 128:192, :] = pack_rope(both[:, 64:]).astype(BF16)
    iw[s] = sw[s]
    iq[s] = sq[s]
    pl.semaphore_wait(bar, len(peers))

    sends = []

    mine = lat.at[c, k, pl.ds(zrow, LAT_PART)]
    rest = lat.at[c, k, pl.ds(LAT_Z, 576 - LAT_Z)]
    for i, r in enumerate(CHIP_PEERS):
        cp = remote(mine, mine, l1s.at[i], l1r.at[k], (chip_peer(r) * 2 + c, f))
        cp.start()
        sends.append(cp)
    for i, r in enumerate(CHIP_PEERS):
        cp = remote(rest, rest, lds.at[i], ldr.at[k], (chip_peer(r) * 2 + c, f))
        cp.start()
        sends.append(cp)
    cp = remote(lat.at[c, k], lat.at[c, k], l3s.at[k], l3r.at[k], other_core)
    cp.start()
    sends.append(cp)
    for i, r in enumerate(SEQ_PEERS):
        p = seq_peer(r)
        cp = remote(sw.at[p], iw.at[s], iws.at[i], iwr.at[s], (p, f))
        cp.start()
        sends.append(cp)
    for i, r in enumerate(CHIP_PEERS):
        q = chip_peer(r)
        piece = lat.at[c, q, pl.ds(zrow, LAT_PART)]
        remote(piece, piece, l1s.at[i], l1r.at[q], other_core).wait_recv()
        for j, dz in enumerate((1, 3, 2)):
            cp = remote(piece, piece, l2s.at[3 * i + j], l2r.at[4 * q + z], (s, h * 4 + z_peer(dz)))
            cp.start()
            sends.append(cp)
    def send_queries(peers):
        for i in peers:
            for e in range(2):
                p = chip_peer(CHIP_PEERS[i]) * 2 + e
                remote(sq.at[p], iq.at[s], iqs.at[2 * i + e], iqr.at[s], (p, f)).start()

    remote(sq.at[k * 2 + 1 - c], iq.at[s], iqs.at[14], iqr.at[s], other_core).start()
    send_queries(range(7))
    for r in CHIP_PEERS:
        block = lat.at[c, chip_peer(r), pl.ds(LAT_Z, 576 - LAT_Z)]
        remote(block, block, lds.at[0], ldr.at[chip_peer(r)], other_core).wait_recv()
    for r in SEQ_PEERS:
        p = seq_peer(r)
        remote(iw.at[p], iw.at[p], iws.at[0], iwr.at[p], other_core).wait_recv()

    for d in range(16):
        wt[0, 32 * d : 32 * d + 32, :] = iw[d, 0:32, :]
        wt[1, 32 * d : 32 * d + 32, :] = iw[d, 32:64, :]
    wtT[0:128, :] = wt[0].astype(F32).T.astype(BF16)
    wtT[128:256, :] = wt[1].astype(F32).T.astype(BF16)

    for i, r in enumerate(CHIP_PEERS):
        q = chip_peer(r)
        for dz in (1, 3, 2):
            zz = z_peer(dz)
            piece = lat.at[c, q, pl.ds(pl.multiple_of(zz * LAT_PART, 16), LAT_PART)]
            remote(piece, piece, l2s.at[0], l2r.at[4 * q + zz], other_core).wait_recv()
        cp = remote(lat.at[c, q], lat.at[c, q], l3s.at[q], l3r.at[q], other_core)
        cp.start()
        sends.append(cp)


    for r in [(0, 0)] + CHIP_PEERS:
        t = chip_peer(r)
        block = lat.at[1 - c, t]
        remote(block, block, l3s.at[0], l3r.at[t], other_core).wait_recv()
        rope = tile_of(lat, t, 512, 576)
        kv = dot(wtT[...], tile_of(lat, t, 0, 512))
        kcT[t, 0:128, :] = kv[:128].astype(BF16)
        kcT[t, 128:192, :] = rope
        vT[t] = kv[128:].astype(BF16)
        kc[t, :, 0:128] = kv[:128].T.astype(BF16)
        kc[t, :, 128:192] = rope.astype(F32).T.astype(BF16)
        v[t] = kv[128:].T.astype(BF16)

    lane = lax.broadcasted_iota(jnp.int32, (1, 256), 1)

    def bias_of(a, b):
        seen = (seg[128 * a] == seg[128 * b]) | (anc[a, b] == 1)
        return jnp.where(seen, 0.0, NEG).astype(F32)

    def pair_index(I, J):
        return I * (I + 1) // 2 + J

    def query_tile(I):
        a0, a1 = iq[2 * I], iq[2 * I + 1]
        qn = jnp.concatenate([a0[0:128], a1[0:128]], axis=0)
        g = jnp.concatenate([a0[192:320], a1[192:320]], axis=0)
        qr = jnp.concatenate(
            [unpack_rope(a0[128:192].astype(F32)), unpack_rope(a1[128:192].astype(F32))], axis=0
        )
        qT = jnp.concatenate([qn.astype(F32).T, qr.T], axis=0).astype(BF16)
        qcs[I] = jnp.concatenate([qn, qr.astype(BF16)], axis=1)
        gcs[I] = g
        gT = g.astype(F32).T
        top = jnp.full((1, 256), NEG, F32)
        for J in range(I + 1):
            scores = dot(kc[J], qT)
            if J < I:
                halves = []
                for b in range(2):
                    bias = jnp.where(
                        lane < 128, bias_of(2 * I, 2 * J + b), bias_of(2 * I + 1, 2 * J + b)
                    )
                    halves.append(scores[128 * b : 128 * b + 128] + bias)
                scores = jnp.concatenate(halves, axis=0)
            else:
                key = lax.broadcasted_iota(jnp.int32, (256, 256), 0)
                query = lax.broadcasted_iota(jnp.int32, (256, 256), 1)
                bias = jnp.where(lane < 128, 0.0, bias_of(2 * I + 1, 2 * I))
                scores = jnp.concatenate([scores[:128] + bias, scores[128:]], axis=0)
                scores = jnp.where(key <= query, scores, NEG)
            sc[J] = scores
            top = jnp.maximum(top, jnp.max(scores, axis=0, keepdims=True))
        top = top * SCALE_LOG2E
        total = jnp.zeros((1, 256), F32)
        oT = jnp.zeros((128, 256), F32)
        for J in range(I + 1):
            weight = jnp.exp2(sc[J] * SCALE_LOG2E - top)
            total = total + jnp.sum(weight, axis=0, keepdims=True)
            sc[J] = weight
            oT = oT + dot(vT[J], weight.astype(BF16))
        inverse = 1.0 / total
        oT = oT * inverse
        delta = jnp.sum(oT * gT, axis=0, keepdims=True)
        gT = gT.astype(BF16)
        dqT = jnp.zeros((192, 256), F32)
        for J in range(I + 1):
            prob = sc[J] * inverse
            ds = (prob * (dot(v[J], gT) - delta)).astype(BF16)
            dss[pair_index(I, J)] = ds
            ps[pair_index(I, J)] = prob.astype(BF16)
            dqT = dqT + dot(kcT[J], ds)
        dqT = dqT * SCALE
        o = oT.T.astype(BF16)
        dqn = dqT[:128].T.astype(BF16)
        dqr = dqT[128:].T
        for e in range(2):
            lo = 128 * e
            so[2 * I + e, 0:128, :] = o[lo : lo + 128]
            so[2 * I + e, 128:256, :] = dqn[lo : lo + 128]
            so[2 * I + e, 256:320, :] = pack_rope(dqr[lo : lo + 128]).astype(BF16)

    def backward_keys(J):
        dk = jnp.zeros((256, 192), F32)
        dv = jnp.zeros((256, 128), F32)
        for I in range(J, TILES):
            dk = dk + dot(dss[pair_index(I, J)], qcs[I])
            dv = dv + dot(ps[pair_index(I, J)], gcs[I])
        dk = dk * SCALE
        dks[...] = dk
        dvs[...] = dv

    def key_grads(J):
        dk = dks[...]
        kv = jnp.concatenate([dk[:, :128], dvs[...]], axis=1)
        kvs[J] = kv.astype(BF16)
        w = jnp.concatenate([wt[0], wt[1]], axis=1)
        lat_grad = dot(w, kv.T.astype(BF16)).astype(BF16)
        rope_grad = dk[:, 128:].T.astype(BF16)
        for e in range(2):
            dl[e, J, 0:512, :] = lat_grad[:, 128 * e : 128 * e + 128]
            dl[e, J, 512:576, :] = rope_grad[:, 128 * e : 128 * e + 128]
        remote(dl.at[1 - c, J], ra.at[J], ras.at[J], rar.at[J], other_core).start()

    def z_rows(base, size, zz):
        return pl.ds(pl.multiple_of(base + zz * size, 16), size)

    def add_cores(J):
        remote(ra.at[J], ra.at[J], ras.at[J], rar.at[J], other_core).wait_recv()
        sa[J] = (dl[c, J].astype(F32) + ra[J].astype(F32)).astype(BF16)
        for j, dz in enumerate((1, 3, 2)):
            zz = z_peer(dz)
            remote(
                sa.at[J, z_rows(0, PART_Z, zz)], rb.at[J, z], rbs.at[3 * J + j], rbr.at[4 * J + z], (s, h * 4 + zz)
            ).start()

        @pl.when(J != k)
        def _():
            remote(
                sa.at[J, pl.ds(ALONG_Z, REST)], ry.at[k], rys.at[J], ryr.at[k], (2 * J + c, f)
            ).start()

    def add_along_z(J):
        acc = sa[J, z_rows(0, PART_Z, z), :].astype(F32)
        for dz in (1, 3, 2):
            zz = z_peer(dz)
            remote(rb.at[J, zz], rb.at[J, zz], rbs.at[0], rbr.at[4 * J + zz], other_core).wait_recv()
            acc = acc + rb[J, zz].astype(F32)
        sb[J] = acc.astype(BF16)

    def tile_at(step):
        far = (step + 6) // 8
        turn = (step + 1) % 3
        dy = far * (1 + 2 * turn - 3 * (turn // 2))
        dx = (1 - far) * step + far * ((step + 1) // 3 - 1)
        return ((y + dy) % 4) * 2 + (x + dx) % 2

    def query_step(step, carry):
        tile = tile_at(step)
        for e in range(2):
            d = 2 * tile + e

            @pl.when(s != d)
            def _():
                remote(iq.at[d], iq.at[d], iqs.at[0], iqr.at[d], other_core).wait_recv()

        for I in range(TILES):

            @pl.when(tile == I)
            def _():
                query_tile(I)

        for e in range(2):
            d = 2 * tile + e

            @pl.when(s != d)
            def _():
                remote(so.at[d], ro.at[s], os.at[d], orr.at[s], (d, f)).start()

        return carry

    lax.fori_loop(0, TILES, query_step, 0)
    def key_step(step, carry):
        tile = tile_at(TILES - 1 - step)
        for J in range(TILES):

            @pl.when(tile == J)
            def _():
                backward_keys(J)

        key_grads(tile)

        @pl.when(step >= LAG)
        def _():
            add_cores(tile_at(TILES - 1 - step + LAG))

        @pl.when(step >= 2 * LAG)
        def _():
            add_along_z(tile_at(TILES - 1 - step + 2 * LAG))

        return carry

    lax.fori_loop(0, TILES, key_step, 0)
    w_grad = jnp.zeros((512, 256), F32)
    for t in range(TILES):
        w_grad = w_grad + dot(tile_of(lat, t, 0, 512), kvs[t])
    w_grad = w_grad.astype(BF16)
    for d in range(16):
        sdw[d, 0:32, :] = w_grad[32 * d : 32 * d + 32, :128]
        sdw[d, 32:64, :] = w_grad[32 * d : 32 * d + 32, 128:]
    for step in range(LAG - 1, -1, -1):
        add_cores(tile_at(step))
    for i, r in enumerate(SEQ_PEERS):
        p = seq_peer(r)
        cp = remote(sdw.at[p], rw.at[s], ws.at[i], wr.at[s], (p, f))
        cp.start()
        sends.append(cp)
    for step in range(2 * LAG - 1, -1, -1):
        add_along_z(tile_at(step))

    for i, r in enumerate(CHIP_PEERS):
        q = chip_peer(r)
        cp = remote(sb.at[q], rc.at[k], rcs.at[i], rcr.at[k], (2 * q + c, f))
        cp.start()
        sends.append(cp)
    acc = sa[k, ALONG_Z:576, :].astype(F32)
    for r in CHIP_PEERS:
        q = chip_peer(r)
        remote(ry.at[q], ry.at[q], rys.at[0], ryr.at[q], other_core).wait_recv()
        acc = acc + ry[q].astype(F32)
    sy[...] = acc.astype(BF16)
    for j, dz in enumerate((1, 3, 2)):
        zz = z_peer(dz)
        cp = remote(sy.at[z_rows(0, PART_REST, zz)], rz.at[z], rzs.at[j], rzr.at[z], (s, h * 4 + zz))
        cp.start()
        sends.append(cp)
    acc = sb[k].astype(F32)
    for r in CHIP_PEERS:
        q = chip_peer(r)
        remote(rc.at[q], rc.at[q], rcs.at[0], rcr.at[q], other_core).wait_recv()
        acc = acc + rc[q].astype(F32)
    part[0:PART_Z, :] = acc.astype(BF16)
    acc = sy[z_rows(0, PART_REST, z), :].astype(F32)
    for dz in (1, 3, 2):
        zz = z_peer(dz)
        remote(rz.at[zz], rz.at[zz], rzs.at[0], rzr.at[zz], other_core).wait_recv()
        acc = acc + rz[zz].astype(F32)
    part[PART_Z:PART, :] = acc.astype(BF16)
    cp = remote(part, other, hs.at[0], hr.at[0], (s, (1 - h) * 4 + z))
    cp.start()
    sends.append(cp)
    cp.wait_recv()
    whole[...] = (part[...].astype(F32) + other[...].astype(F32)).astype(BF16)
    for j, dz in enumerate((1, 3, 2)):
        cp = remote(whole, fe.at[z], es.at[j], er.at[z], (s, h * 4 + z_peer(dz)))
        cp.start()
        sends.append(cp)
    kept = [
        pltpu.make_async_copy(src, dst, own.at[i])
        for i, (src, dst) in enumerate(
            [(so.at[s], ro.at[s]), (sdw.at[s], rw.at[s]), (whole, fe.at[z])]
        )
    ]
    for cp in kept:
        cp.start()

    for r in SEQ_PEERS:
        p = seq_peer(r)
        remote(ro.at[p], ro.at[p], os.at[0], orr.at[p], other_core).wait_recv()
        remote(rw.at[p], rw.at[p], ws.at[0], wr.at[p], other_core).wait_recv()
        remote(so.at[p], so.at[p], os.at[p], orr.at[p], other_core).wait_send()
    for dz in (1, 3, 2):
        zz = z_peer(dz)
        remote(whole, fe.at[zz], es.at[0], er.at[zz], other_core).wait_recv()
    for cp in kept:
        cp.wait()
    for cp in sends:
        cp.wait_send()
    for i in range(15):
        remote(sq.at[0], sq.at[0], iqs.at[i], iqr.at[0], other_core).wait_send()
    for J in range(TILES):
        remote(ra.at[J], ra.at[J], ras.at[J], rar.at[J], other_core).wait_send()
        for j in range(3):
            remote(rb.at[J, 0], rb.at[J, 0], rbs.at[3 * J + j], rbr.at[0], other_core).wait_send()

        @pl.when(J != k)
        def _():
            remote(ry.at[0], ry.at[0], rys.at[J], ryr.at[0], other_core).wait_send()


def unpack(
    ro_hbm, rw_hbm, fe_hbm, out, dqn, dqr, dlat, dkr, duk, duv, ro, rw, fe, sems
):
    loads = [
        pltpu.make_async_copy(src, dst, sems.at[i])
        for i, (src, dst) in enumerate([(ro_hbm, ro), (rw_hbm, rw), (fe_hbm, fe)])
    ]
    for cp in loads:
        cp.start()
    for cp in loads:
        cp.wait()
    for d in range(16):
        cols = slice(128 * d, 128 * d + 128)
        out[:, cols] = ro[d, 0:128, :]
        dqn[:, cols] = ro[d, 128:256, :]
        duk[:, cols] = rw[d, 0:32, :].astype(F32)
        duv[:, cols] = rw[d, 32:64, :].astype(F32)
    for pair in range(8):
        both = [unpack_rope(ro[2 * pair + e, 256:320, :].astype(F32)) for e in range(2)]
        dqr[:, 128 * pair : 128 * pair + 128] = jnp.concatenate(both, axis=1).astype(BF16)
    for z in range(4):
        dlat[PART_Z * z : PART_Z * z + PART_Z, :] = fe[z, 0:PART_Z, :]
        rest = fe[z, PART_Z:PART, :]
        lo = ALONG_Z + PART_REST * z
        if lo < 512:
            dlat[lo : lo + PART_REST, :] = rest
        else:
            dkr[lo - 512 : lo - 512 + PART_REST, :] = rest


def on_device(q_nope, q_rope, latent_t, k_rope_t, w_uk, w_uv, grad_out, seg_ids, anc_flags):
    vmem = pl.BlockSpec(memory_space=pltpu.VMEM)
    smem = pl.BlockSpec(memory_space=pltpu.SMEM)
    anywhere = pl.BlockSpec(memory_space=pl.ANY)
    dma = pltpu.SemaphoreType.DMA
    sem_counts = [7, 3, 7, 8, 7, 8, 21, 32, 8, 8, 15, 16, 15, 16, 16, 16, 8, 8, 24, 32, 7, 8]
    sem_counts += [8, 8, 3, 4, 1, 1, 15, 16, 3, 4]
    parts = pl.pallas_call(
        fused,
        out_shape=[
            jax.ShapeDtypeStruct((16, 320, 128), BF16),
            jax.ShapeDtypeStruct((16, 64, 128), BF16),
            jax.ShapeDtypeStruct((4, PART, 128), BF16),
        ],
        in_specs=[smem, smem] + [anywhere] * 7,
        out_specs=[anywhere] * 3,
        scratch_shapes=[
            pltpu.VMEM((128, 2048), BF16),
            pltpu.VMEM((128, 1024), BF16),
            pltpu.VMEM((32, 2048), BF16),
            pltpu.VMEM((32, 2048), BF16),
            pltpu.VMEM((128, 2048), BF16),
            pltpu.VMEM((2, 8, 576, 128), BF16),
            pltpu.VMEM((16, 64, 128), BF16),
            pltpu.VMEM((16, 64, 128), BF16),
            pltpu.VMEM((16, 320, 128), BF16),
            pltpu.VMEM((16, 320, 128), BF16),
            pltpu.VMEM((2, 512, 128), BF16),
            pltpu.VMEM((256, 512), BF16),
            pltpu.VMEM((8, 192, 256), BF16),
            pltpu.VMEM((8, 128, 256), BF16),
            pltpu.VMEM((8, 256, 192), BF16),
            pltpu.VMEM((8, 256, 128), BF16),
            pltpu.VMEM((8, 256, 256), F32),
            pltpu.VMEM((36, 256, 256), BF16),
            pltpu.VMEM((36, 256, 256), BF16),
            pltpu.VMEM((8, 256, 192), BF16),
            pltpu.VMEM((8, 256, 128), BF16),
            pltpu.VMEM((256, 192), F32),
            pltpu.VMEM((256, 128), F32),
            pltpu.VMEM((8, 256, 256), BF16),
            pltpu.VMEM((16, 320, 128), BF16),
            pltpu.VMEM((16, 64, 128), BF16),
            pltpu.VMEM((2, 8, 576, 128), BF16),
            pltpu.VMEM((8, 576, 128), BF16),
            pltpu.VMEM((8, 576, 128), BF16),
            pltpu.VMEM((8, 4, PART_Z, 128), BF16),
            pltpu.VMEM((8, PART_Z, 128), BF16),
            pltpu.VMEM((8, PART_Z, 128), BF16),
            pltpu.VMEM((8, REST, 128), BF16),
            pltpu.VMEM((REST, 128), BF16),
            pltpu.VMEM((4, PART_REST, 128), BF16),
            pltpu.VMEM((PART, 128), BF16),
            pltpu.VMEM((PART, 128), BF16),
            pltpu.VMEM((PART, 128), BF16),
        ]
        + [dma((n,)) for n in sem_counts],
        compiler_params=pltpu.CompilerParams(
            collective_id=0, has_side_effects=True, vmem_limit_bytes=56 * 1024 * 1024
        ),
        name="attention_exchange",
    )(seg_ids, anc_flags, q_nope, q_rope, latent_t, k_rope_t, w_uk, w_uv, grad_out)
    bf, fl = BF16, F32
    return pl.pallas_call(
        unpack,
        out_shape=[
            jax.ShapeDtypeStruct((128, 2048), bf),
            jax.ShapeDtypeStruct((128, 2048), bf),
            jax.ShapeDtypeStruct((128, 1024), bf),
            jax.ShapeDtypeStruct((512, 128), bf),
            jax.ShapeDtypeStruct((64, 128), bf),
            jax.ShapeDtypeStruct((32, 2048), fl),
            jax.ShapeDtypeStruct((32, 2048), fl),
        ],
        in_specs=[anywhere] * 3,
        out_specs=[vmem] * 7,
        scratch_shapes=[
            pltpu.VMEM((16, 320, 128), bf),
            pltpu.VMEM((16, 64, 128), bf),
            pltpu.VMEM((4, PART, 128), bf),
            dma((3,)),
        ],
        compiler_params=pltpu.CompilerParams(vmem_limit_bytes=60 * 1024 * 1024),
        name="unpack",
    )(*parts)


def solution(mesh):
    placed = (
        P("seq", "fsdp"),
        P("seq", "fsdp"),
        P(None, "seq"),
        P(None, "seq"),
        P("seq", "fsdp"),
        P("seq", "fsdp"),
        P("seq", "fsdp"),
        P(),
        P(),
    )
    return jax.shard_map(
        on_device,
        mesh=mesh,
        in_specs=placed,
        out_specs=(
            P("seq", "fsdp"),
            P("seq", "fsdp"),
            P("seq", "fsdp"),
            P(None, "seq"),
            P(None, "seq"),
            P("seq", "fsdp"),
            P("seq", "fsdp"),
        ),
        check_vma=False,
    )
```

```python
import functools
import math

import jax
import jax.numpy as jnp
from jax import lax
from jax.experimental import pallas as pl
from jax.experimental.pallas import tpu as pltpu
from jax.sharding import PartitionSpec as P

F32, BF16 = jnp.float32, jnp.bfloat16
MESH = pl.DeviceIdType.MESH
NEG = -1e30
SCALE = 1.0 / math.sqrt(192.0)
SCALE_LOG2E = SCALE * math.log2(math.e)
TILES = 8
LAG = 3
LAT_Z = 512
LAT_PART = LAT_Z // 4
PART = 144
ALONG_Z = 320
PART_Z = ALONG_Z // 4
REST = 576 - ALONG_Z
PART_REST = REST // 4

SEQ_PEERS = [(dy, dx, dc) for dy in (0, 3, 1, 2) for dx in (0, 1) for dc in (0, 1)][1:]
CHIP_PEERS = [(0, 1), (1, 0), (3, 0), (2, 0), (1, 1), (3, 1), (2, 1)]


def dot(left, right):
    return lax.dot_general(left, right, (((1,), (0,)), ((), ())), preferred_element_type=F32)


def unpack_rope(x):
    return jnp.concatenate([x[:, :64], x[:, 64:]], axis=0)


def pack_rope(x):
    return jnp.concatenate([x[:64], x[64:]], axis=1)


def tile_of(lat, t, lo, hi):
    return jnp.concatenate([lat[0, t, lo:hi, :], lat[1, t, lo:hi, :]], axis=1)


def fused(
    seg, anc, qn_hbm, qr_hbm, lt_hbm, kr_hbm, uk_hbm, uv_hbm, g_hbm,
    ro, rw, fe,
    qn_in, qr_in, uk_in, uv_in, g_in,
    lat, sw, iw, sq, iq, wt, wtT, kcT, vT, kc, v, sc, dss, ps, qcs, gcs, dks, dvs, kvs, so, sdw, dl, ra, sa,
    rb, sb, rc, ry, sy, rz, part, other, whole,
    ins, own, l1s, l1r, lds, ldr, l2s, l2r, l3s, l3r, iws, iwr, iqs, iqr, os, orr, ras, rar, rbs, rbr, rcs, rcr,
    rys, ryr, rzs, rzr, hs, hr, ws, wr, es, er,
):
    s, f = lax.axis_index("seq"), lax.axis_index("fsdp")
    y, x, c = s // 4, (s // 2) % 2, s % 2
    k = s // 2
    h, z = f // 4, f % 4

    def seq_peer(rel):
        return ((y + rel[0]) % 4) * 4 + ((x + rel[1]) % 2) * 2 + (c + rel[2]) % 2

    def chip_peer(rel):
        return ((y + rel[0]) % 4) * 2 + (x + rel[1]) % 2

    def z_peer(dz):
        return (z + dz) % 4

    other_core = (k * 2 + 1 - c, f)
    zrow = pl.multiple_of(z * LAT_PART, 16)

    def remote(src, dst, ssem, rsem, device):
        return pltpu.make_async_remote_copy(
            src_ref=src, dst_ref=dst, send_sem=ssem, recv_sem=rsem, device_id=device, device_id_type=MESH
        )

    loads = [
        pltpu.make_async_copy(src, dst, ins.at[i])
        for i, (src, dst) in enumerate(
            [
                (lt_hbm, lat.at[c, k, pl.ds(0, 512)]),
                (kr_hbm, lat.at[c, k, pl.ds(512, 64)]),
                (uk_hbm, uk_in),
                (uv_hbm, uv_in),
                (qn_hbm, qn_in),
                (qr_hbm, qr_in),
                (g_hbm, g_in),
            ]
        )
    ]
    for cp in loads:
        cp.start()

    bar = pltpu.get_barrier_semaphore()
    peers = [(seq_peer(r), f) for r in SEQ_PEERS]
    peers += [(s, h * 4 + z_peer(dz)) for dz in (1, 2, 3)]
    peers += [(s, (1 - h) * 4 + z)]
    for p in peers:
        pl.semaphore_signal(bar, inc=1, device_id=p, device_id_type=MESH)

    for cp in loads:
        cp.wait()
    for d in range(16):
        sw[d, 0:32, :] = uk_in[:, 128 * d : 128 * d + 128]
        sw[d, 32:64, :] = uv_in[:, 128 * d : 128 * d + 128]
        sq[d, 0:128, :] = qn_in[:, 128 * d : 128 * d + 128]
        sq[d, 192:320, :] = g_in[:, 128 * d : 128 * d + 128]
    for pair in range(8):
        both = qr_in[:, 128 * pair : 128 * pair + 128].astype(F32)
        sq[2 * pair, 128:192, :] = pack_rope(both[:, :64]).astype(BF16)
        sq[2 * pair + 1, 128:192, :] = pack_rope(both[:, 64:]).astype(BF16)
    iw[s] = sw[s]
    iq[s] = sq[s]
    pl.semaphore_wait(bar, len(peers))

    sends = []

    mine = lat.at[c, k, pl.ds(zrow, LAT_PART)]
    rest = lat.at[c, k, pl.ds(LAT_Z, 576 - LAT_Z)]
    for i, r in enumerate(CHIP_PEERS):
        cp = remote(mine, mine, l1s.at[i], l1r.at[k], (chip_peer(r) * 2 + c, f))
        cp.start()
        sends.append(cp)
    for i, r in enumerate(CHIP_PEERS):
        cp = remote(rest, rest, lds.at[i], ldr.at[k], (chip_peer(r) * 2 + c, f))
        cp.start()
        sends.append(cp)
    cp = remote(lat.at[c, k], lat.at[c, k], l3s.at[k], l3r.at[k], other_core)
    cp.start()
    sends.append(cp)
    for i, r in enumerate(SEQ_PEERS):
        p = seq_peer(r)
        cp = remote(sw.at[p], iw.at[s], iws.at[i], iwr.at[s], (p, f))
        cp.start()
        sends.append(cp)
    for i, r in enumerate(CHIP_PEERS):
        q = chip_peer(r)
        piece = lat.at[c, q, pl.ds(zrow, LAT_PART)]
        remote(piece, piece, l1s.at[i], l1r.at[q], other_core).wait_recv()
        for j, dz in enumerate((1, 3, 2)):
            cp = remote(piece, piece, l2s.at[3 * i + j], l2r.at[4 * q + z], (s, h * 4 + z_peer(dz)))
            cp.start()
            sends.append(cp)
    def send_queries(peers):
        for i in peers:
            for e in range(2):
                p = chip_peer(CHIP_PEERS[i]) * 2 + e
                remote(sq.at[p], iq.at[s], iqs.at[2 * i + e], iqr.at[s], (p, f)).start()

    remote(sq.at[k * 2 + 1 - c], iq.at[s], iqs.at[14], iqr.at[s], other_core).start()
    send_queries(range(7))
    for r in CHIP_PEERS:
        block = lat.at[c, chip_peer(r), pl.ds(LAT_Z, 576 - LAT_Z)]
        remote(block, block, lds.at[0], ldr.at[chip_peer(r)], other_core).wait_recv()
    for r in SEQ_PEERS:
        p = seq_peer(r)
        remote(iw.at[p], iw.at[p], iws.at[0], iwr.at[p], other_core).wait_recv()

    for d in range(16):
        wt[0, 32 * d : 32 * d + 32, :] = iw[d, 0:32, :]
        wt[1, 32 * d : 32 * d + 32, :] = iw[d, 32:64, :]
    wtT[0:128, :] = wt[0].astype(F32).T.astype(BF16)
    wtT[128:256, :] = wt[1].astype(F32).T.astype(BF16)

    for i, r in enumerate(CHIP_PEERS):
        q = chip_peer(r)
        for dz in (1, 3, 2):
            zz = z_peer(dz)
            piece = lat.at[c, q, pl.ds(pl.multiple_of(zz * LAT_PART, 16), LAT_PART)]
            remote(piece, piece, l2s.at[0], l2r.at[4 * q + zz], other_core).wait_recv()
        cp = remote(lat.at[c, q], lat.at[c, q], l3s.at[q], l3r.at[q], other_core)
        cp.start()
        sends.append(cp)


    for r in [(0, 0)] + CHIP_PEERS:
        t = chip_peer(r)
        block = lat.at[1 - c, t]
        remote(block, block, l3s.at[0], l3r.at[t], other_core).wait_recv()
        rope = tile_of(lat, t, 512, 576)
        kv = dot(wtT[...], tile_of(lat, t, 0, 512))
        kcT[t, 0:128, :] = kv[:128].astype(BF16)
        kcT[t, 128:192, :] = rope
        vT[t] = kv[128:].astype(BF16)
        kc[t, :, 0:128] = kv[:128].T.astype(BF16)
        kc[t, :, 128:192] = rope.astype(F32).T.astype(BF16)
        v[t] = kv[128:].T.astype(BF16)

    lane = lax.broadcasted_iota(jnp.int32, (1, 256), 1)

    def bias_of(a, b):
        seen = (seg[128 * a] == seg[128 * b]) | (anc[a, b] == 1)
        return jnp.where(seen, 0.0, NEG).astype(F32)

    def pair_index(I, J):
        return I * (I + 1) // 2 + J

    def query_tile(I):
        a0, a1 = iq[2 * I], iq[2 * I + 1]
        qn = jnp.concatenate([a0[0:128], a1[0:128]], axis=0)
        g = jnp.concatenate([a0[192:320], a1[192:320]], axis=0)
        qr = jnp.concatenate(
            [unpack_rope(a0[128:192].astype(F32)), unpack_rope(a1[128:192].astype(F32))], axis=0
        )
        qT = jnp.concatenate([qn.astype(F32).T, qr.T], axis=0).astype(BF16)
        qcs[I] = jnp.concatenate([qn, qr.astype(BF16)], axis=1)
        gcs[I] = g
        gT = g.astype(F32).T
        top = jnp.full((1, 256), NEG, F32)
        for J in range(I + 1):
            scores = dot(kc[J], qT)
            if J < I:
                halves = []
                for b in range(2):
                    bias = jnp.where(
                        lane < 128, bias_of(2 * I, 2 * J + b), bias_of(2 * I + 1, 2 * J + b)
                    )
                    halves.append(scores[128 * b : 128 * b + 128] + bias)
                scores = jnp.concatenate(halves, axis=0)
            else:
                key = lax.broadcasted_iota(jnp.int32, (256, 256), 0)
                query = lax.broadcasted_iota(jnp.int32, (256, 256), 1)
                bias = jnp.where(lane < 128, 0.0, bias_of(2 * I + 1, 2 * I))
                scores = jnp.concatenate([scores[:128] + bias, scores[128:]], axis=0)
                scores = jnp.where(key <= query, scores, NEG)
            sc[J] = scores
            top = jnp.maximum(top, jnp.max(scores, axis=0, keepdims=True))
        top = top * SCALE_LOG2E
        total = jnp.zeros((1, 256), F32)
        oT = jnp.zeros((128, 256), F32)
        for J in range(I + 1):
            weight = jnp.exp2(sc[J] * SCALE_LOG2E - top)
            total = total + jnp.sum(weight, axis=0, keepdims=True)
            sc[J] = weight
            oT = oT + dot(vT[J], weight.astype(BF16))
        inverse = 1.0 / total
        oT = oT * inverse
        delta = jnp.sum(oT * gT, axis=0, keepdims=True)
        gT = gT.astype(BF16)
        dqT = jnp.zeros((192, 256), F32)
        for J in range(I + 1):
            prob = sc[J] * inverse
            ds = (prob * (dot(v[J], gT) - delta)).astype(BF16)
            dss[pair_index(I, J)] = ds
            ps[pair_index(I, J)] = prob.astype(BF16)
            dqT = dqT + dot(kcT[J], ds)
        dqT = dqT * SCALE
        o = oT.T.astype(BF16)
        dqn = dqT[:128].T.astype(BF16)
        dqr = dqT[128:].T
        for e in range(2):
            lo = 128 * e
            so[2 * I + e, 0:128, :] = o[lo : lo + 128]
            so[2 * I + e, 128:256, :] = dqn[lo : lo + 128]
            so[2 * I + e, 256:320, :] = pack_rope(dqr[lo : lo + 128]).astype(BF16)

    def backward_keys(J):
        dk = jnp.zeros((256, 192), F32)
        dv = jnp.zeros((256, 128), F32)
        for I in range(J, TILES):
            dk = dk + dot(dss[pair_index(I, J)], qcs[I])
            dv = dv + dot(ps[pair_index(I, J)], gcs[I])
        dk = dk * SCALE
        dks[...] = dk
        dvs[...] = dv

    def key_grads(J):
        dk = dks[...]
        kv = jnp.concatenate([dk[:, :128], dvs[...]], axis=1)
        kvs[J] = kv.astype(BF16)
        w = jnp.concatenate([wt[0], wt[1]], axis=1)
        lat_grad = dot(w, kv.T.astype(BF16)).astype(BF16)
        rope_grad = dk[:, 128:].T.astype(BF16)
        for e in range(2):
            dl[e, J, 0:512, :] = lat_grad[:, 128 * e : 128 * e + 128]
            dl[e, J, 512:576, :] = rope_grad[:, 128 * e : 128 * e + 128]
        remote(dl.at[1 - c, J], ra.at[J], ras.at[J], rar.at[J], other_core).start()

    def z_rows(base, size, zz):
        return pl.ds(pl.multiple_of(base + zz * size, 16), size)

    def add_cores(J):
        remote(ra.at[J], ra.at[J], ras.at[J], rar.at[J], other_core).wait_recv()
        sa[J] = (dl[c, J].astype(F32) + ra[J].astype(F32)).astype(BF16)
        for j, dz in enumerate((1, 3, 2)):
            zz = z_peer(dz)
            remote(
                sa.at[J, z_rows(0, PART_Z, zz)], rb.at[J, z], rbs.at[3 * J + j], rbr.at[4 * J + z], (s, h * 4 + zz)
            ).start()

        @pl.when(J != k)
        def _():
            remote(
                sa.at[J, pl.ds(ALONG_Z, REST)], ry.at[k], rys.at[J], ryr.at[k], (2 * J + c, f)
            ).start()

    def add_along_z(J):
        acc = sa[J, z_rows(0, PART_Z, z), :].astype(F32)
        for dz in (1, 3, 2):
            zz = z_peer(dz)
            remote(rb.at[J, zz], rb.at[J, zz], rbs.at[0], rbr.at[4 * J + zz], other_core).wait_recv()
            acc = acc + rb[J, zz].astype(F32)
        sb[J] = acc.astype(BF16)

    def tile_at(step):
        far = (step + 6) // 8
        turn = (step + 1) % 3
        dy = far * (1 + 2 * turn - 3 * (turn // 2))
        dx = (1 - far) * step + far * ((step + 1) // 3 - 1)
        return ((y + dy) % 4) * 2 + (x + dx) % 2

    def query_step(step, carry):
        tile = tile_at(step)
        for e in range(2):
            d = 2 * tile + e

            @pl.when(s != d)
            def _():
                remote(iq.at[d], iq.at[d], iqs.at[0], iqr.at[d], other_core).wait_recv()

        for I in range(TILES):

            @pl.when(tile == I)
            def _():
                query_tile(I)

        for e in range(2):
            d = 2 * tile + e

            @pl.when(s != d)
            def _():
                remote(so.at[d], ro.at[s], os.at[d], orr.at[s], (d, f)).start()

        return carry

    lax.fori_loop(0, TILES, query_step, 0)
    def key_step(step, carry):
        tile = tile_at(TILES - 1 - step)
        for J in range(TILES):

            @pl.when(tile == J)
            def _():
                backward_keys(J)

        key_grads(tile)

        @pl.when(step >= LAG)
        def _():
            add_cores(tile_at(TILES - 1 - step + LAG))

        @pl.when(step >= 2 * LAG)
        def _():
            add_along_z(tile_at(TILES - 1 - step + 2 * LAG))

        return carry

    lax.fori_loop(0, TILES, key_step, 0)
    w_grad = jnp.zeros((512, 256), F32)
    for t in range(TILES):
        w_grad = w_grad + dot(tile_of(lat, t, 0, 512), kvs[t])
    w_grad = w_grad.astype(BF16)
    for d in range(16):
        sdw[d, 0:32, :] = w_grad[32 * d : 32 * d + 32, :128]
        sdw[d, 32:64, :] = w_grad[32 * d : 32 * d + 32, 128:]
    for step in range(LAG - 1, -1, -1):
        add_cores(tile_at(step))
    for i, r in enumerate(SEQ_PEERS):
        p = seq_peer(r)
        cp = remote(sdw.at[p], rw.at[s], ws.at[i], wr.at[s], (p, f))
        cp.start()
        sends.append(cp)
    for step in range(2 * LAG - 1, -1, -1):
        add_along_z(tile_at(step))

    for i, r in enumerate(CHIP_PEERS):
        q = chip_peer(r)
        cp = remote(sb.at[q], rc.at[k], rcs.at[i], rcr.at[k], (2 * q + c, f))
        cp.start()
        sends.append(cp)
    acc = sa[k, ALONG_Z:576, :].astype(F32)
    for r in CHIP_PEERS:
        q = chip_peer(r)
        remote(ry.at[q], ry.at[q], rys.at[0], ryr.at[q], other_core).wait_recv()
        acc = acc + ry[q].astype(F32)
    sy[...] = acc.astype(BF16)
    for j, dz in enumerate((1, 3, 2)):
        zz = z_peer(dz)
        cp = remote(sy.at[z_rows(0, PART_REST, zz)], rz.at[z], rzs.at[j], rzr.at[z], (s, h * 4 + zz))
        cp.start()
        sends.append(cp)
    acc = sb[k].astype(F32)
    for r in CHIP_PEERS:
        q = chip_peer(r)
        remote(rc.at[q], rc.at[q], rcs.at[0], rcr.at[q], other_core).wait_recv()
        acc = acc + rc[q].astype(F32)
    part[0:PART_Z, :] = acc.astype(BF16)
    acc = sy[z_rows(0, PART_REST, z), :].astype(F32)
    for dz in (1, 3, 2):
        zz = z_peer(dz)
        remote(rz.at[zz], rz.at[zz], rzs.at[0], rzr.at[zz], other_core).wait_recv()
        acc = acc + rz[zz].astype(F32)
    part[PART_Z:PART, :] = acc.astype(BF16)
    cp = remote(part, other, hs.at[0], hr.at[0], (s, (1 - h) * 4 + z))
    cp.start()
    sends.append(cp)
    cp.wait_recv()
    whole[...] = (part[...].astype(F32) + other[...].astype(F32)).astype(BF16)
    for j, dz in enumerate((1, 3, 2)):
        cp = remote(whole, fe.at[z], es.at[j], er.at[z], (s, h * 4 + z_peer(dz)))
        cp.start()
        sends.append(cp)
    kept = [
        pltpu.make_async_copy(src, dst, own.at[i])
        for i, (src, dst) in enumerate(
            [(so.at[s], ro.at[s]), (sdw.at[s], rw.at[s]), (whole, fe.at[z])]
        )
    ]
    for cp in kept:
        cp.start()

    for r in SEQ_PEERS:
        p = seq_peer(r)
        remote(ro.at[p], ro.at[p], os.at[0], orr.at[p], other_core).wait_recv()
        remote(rw.at[p], rw.at[p], ws.at[0], wr.at[p], other_core).wait_recv()
        remote(so.at[p], so.at[p], os.at[p], orr.at[p], other_core).wait_send()
    for dz in (1, 3, 2):
        zz = z_peer(dz)
        remote(whole, fe.at[zz], es.at[0], er.at[zz], other_core).wait_recv()
    for cp in kept:
        cp.wait()
    for cp in sends:
        cp.wait_send()
    for i in range(15):
        remote(sq.at[0], sq.at[0], iqs.at[i], iqr.at[0], other_core).wait_send()
    for J in range(TILES):
        remote(ra.at[J], ra.at[J], ras.at[J], rar.at[J], other_core).wait_send()
        for j in range(3):
            remote(rb.at[J, 0], rb.at[J, 0], rbs.at[3 * J + j], rbr.at[0], other_core).wait_send()

        @pl.when(J != k)
        def _():
            remote(ry.at[0], ry.at[0], rys.at[J], ryr.at[0], other_core).wait_send()


def unpack(
    ro_hbm, rw_hbm, fe_hbm, out, dqn, dqr, dlat, dkr, duk, duv, ro, rw, fe, sems
):
    loads = [pltpu.make_async_copy(rw_hbm, rw, sems.at[0]), pltpu.make_async_copy(fe_hbm, fe, sems.at[1])]
    for part in range(4):
        heads = pl.ds(4 * part, 4)
        loads.append(pltpu.make_async_copy(ro_hbm.at[heads], ro.at[heads], sems.at[2 + part]))
    for cp in loads:
        cp.start()
    loads[0].wait()
    for d in range(16):
        cols = slice(128 * d, 128 * d + 128)
        duk[:, cols] = rw[d, 0:32, :].astype(F32)
        duv[:, cols] = rw[d, 32:64, :].astype(F32)
    loads[1].wait()
    for z in range(4):
        dlat[PART_Z * z : PART_Z * z + PART_Z, :] = fe[z, 0:PART_Z, :]
        rest = fe[z, PART_Z:PART, :]
        lo = ALONG_Z + PART_REST * z
        if lo < 512:
            dlat[lo : lo + PART_REST, :] = rest
        else:
            dkr[lo - 512 : lo - 512 + PART_REST, :] = rest
    for part in range(4):
        loads[2 + part].wait()
        for d in range(4 * part, 4 * part + 4):
            cols = slice(128 * d, 128 * d + 128)
            out[:, cols] = ro[d, 0:128, :]
            dqn[:, cols] = ro[d, 128:256, :]
        for pair in range(2 * part, 2 * part + 2):
            both = [unpack_rope(ro[2 * pair + e, 256:320, :].astype(F32)) for e in range(2)]
            dqr[:, 128 * pair : 128 * pair + 128] = jnp.concatenate(both, axis=1).astype(BF16)


def on_device(q_nope, q_rope, latent_t, k_rope_t, w_uk, w_uv, grad_out, seg_ids, anc_flags):
    vmem = pl.BlockSpec(memory_space=pltpu.VMEM)
    smem = pl.BlockSpec(memory_space=pltpu.SMEM)
    anywhere = pl.BlockSpec(memory_space=pl.ANY)
    dma = pltpu.SemaphoreType.DMA
    sem_counts = [7, 3, 7, 8, 7, 8, 21, 32, 8, 8, 15, 16, 15, 16, 16, 16, 8, 8, 24, 32, 7, 8]
    sem_counts += [8, 8, 3, 4, 1, 1, 15, 16, 3, 4]
    parts = pl.pallas_call(
        fused,
        out_shape=[
            jax.ShapeDtypeStruct((16, 320, 128), BF16),
            jax.ShapeDtypeStruct((16, 64, 128), BF16),
            jax.ShapeDtypeStruct((4, PART, 128), BF16),
        ],
        in_specs=[smem, smem] + [anywhere] * 7,
        out_specs=[anywhere] * 3,
        scratch_shapes=[
            pltpu.VMEM((128, 2048), BF16),
            pltpu.VMEM((128, 1024), BF16),
            pltpu.VMEM((32, 2048), BF16),
            pltpu.VMEM((32, 2048), BF16),
            pltpu.VMEM((128, 2048), BF16),
            pltpu.VMEM((2, 8, 576, 128), BF16),
            pltpu.VMEM((16, 64, 128), BF16),
            pltpu.VMEM((16, 64, 128), BF16),
            pltpu.VMEM((16, 320, 128), BF16),
            pltpu.VMEM((16, 320, 128), BF16),
            pltpu.VMEM((2, 512, 128), BF16),
            pltpu.VMEM((256, 512), BF16),
            pltpu.VMEM((8, 192, 256), BF16),
            pltpu.VMEM((8, 128, 256), BF16),
            pltpu.VMEM((8, 256, 192), BF16),
            pltpu.VMEM((8, 256, 128), BF16),
            pltpu.VMEM((8, 256, 256), F32),
            pltpu.VMEM((36, 256, 256), BF16),
            pltpu.VMEM((36, 256, 256), BF16),
            pltpu.VMEM((8, 256, 192), BF16),
            pltpu.VMEM((8, 256, 128), BF16),
            pltpu.VMEM((256, 192), F32),
            pltpu.VMEM((256, 128), F32),
            pltpu.VMEM((8, 256, 256), BF16),
            pltpu.VMEM((16, 320, 128), BF16),
            pltpu.VMEM((16, 64, 128), BF16),
            pltpu.VMEM((2, 8, 576, 128), BF16),
            pltpu.VMEM((8, 576, 128), BF16),
            pltpu.VMEM((8, 576, 128), BF16),
            pltpu.VMEM((8, 4, PART_Z, 128), BF16),
            pltpu.VMEM((8, PART_Z, 128), BF16),
            pltpu.VMEM((8, PART_Z, 128), BF16),
            pltpu.VMEM((8, REST, 128), BF16),
            pltpu.VMEM((REST, 128), BF16),
            pltpu.VMEM((4, PART_REST, 128), BF16),
            pltpu.VMEM((PART, 128), BF16),
            pltpu.VMEM((PART, 128), BF16),
            pltpu.VMEM((PART, 128), BF16),
        ]
        + [dma((n,)) for n in sem_counts],
        compiler_params=pltpu.CompilerParams(
            collective_id=0, has_side_effects=True, vmem_limit_bytes=56 * 1024 * 1024
        ),
        name="attention_exchange",
    )(seg_ids, anc_flags, q_nope, q_rope, latent_t, k_rope_t, w_uk, w_uv, grad_out)
    bf, fl = BF16, F32
    return pl.pallas_call(
        unpack,
        out_shape=[
            jax.ShapeDtypeStruct((128, 2048), bf),
            jax.ShapeDtypeStruct((128, 2048), bf),
            jax.ShapeDtypeStruct((128, 1024), bf),
            jax.ShapeDtypeStruct((512, 128), bf),
            jax.ShapeDtypeStruct((64, 128), bf),
            jax.ShapeDtypeStruct((32, 2048), fl),
            jax.ShapeDtypeStruct((32, 2048), fl),
        ],
        in_specs=[anywhere] * 3,
        out_specs=[vmem] * 7,
        scratch_shapes=[
            pltpu.VMEM((16, 320, 128), bf),
            pltpu.VMEM((16, 64, 128), bf),
            pltpu.VMEM((4, PART, 128), bf),
            dma((6,)),
        ],
        compiler_params=pltpu.CompilerParams(vmem_limit_bytes=60 * 1024 * 1024),
        name="unpack",
    )(*parts)


def solution(mesh):
    placed = (
        P("seq", "fsdp"),
        P("seq", "fsdp"),
        P(None, "seq"),
        P(None, "seq"),
        P("seq", "fsdp"),
        P("seq", "fsdp"),
        P("seq", "fsdp"),
        P(),
        P(),
    )
    return jax.shard_map(
        on_device,
        mesh=mesh,
        in_specs=placed,
        out_specs=(
            P("seq", "fsdp"),
            P("seq", "fsdp"),
            P("seq", "fsdp"),
            P(None, "seq"),
            P(None, "seq"),
            P("seq", "fsdp"),
            P("seq", "fsdp"),
        ),
        check_vma=False,
    )
```
